32 devices in a mesh: groups: 2 (over y), expert: 16 (over z, x, core), dp: 1.
Axes of the slice: x: 2, y: 2, z: 4, core: 2. Of those that a mesh axis runs over, the one named last changes fastest.
Arguments:
- tokens: bfloat16 [4096, 1024], P(('groups', 'expert', 'dp')), parts along dimension 0, may hold values from -6 to 6
- cotangent: bfloat16 [4096, 1024], P(('groups', 'expert', 'dp')), parts along dimension 0, may hold values from -6 to 6
- routes: int32 [4096, 8], P(('groups', 'expert', 'dp')), parts along dimension 0, may hold values from 0 to 15, all different within a row; in each aligned block of 128 rows (0 to 127, 128 to 255, ...) at most 64 rows name the same one
- combine: float32 [4096, 8], P(('groups', 'expert', 'dp')), parts along dimension 0, may hold values from 0.2 to 1
- w_gate: bfloat16 [16, 1024, 384], P('expert'), may hold values from -0.1875 to 0.1875
- w_up: bfloat16 [16, 1024, 384], P('expert'), may hold values from -0.1875 to 0.1875
- w_down: bfloat16 [16, 1024, 384], P('expert'), may hold values from -0.3125 to 0.3125
Outputs:
- mixed: bfloat16 [4096, 1024], P(('groups', 'expert', 'dp')), parts along dimension 0
- grad_tokens: bfloat16 [4096, 1024], P(('groups', 'expert', 'dp')), parts along dimension 0
- grad_gate: bfloat16 [32, 1024, 384], P(('groups', 'expert'), 'dp'), parts along dimension 0
- grad_up: bfloat16 [32, 1024, 384], P(('groups', 'expert'), 'dp'), parts along dimension 0
- grad_down: bfloat16 [32, 1024, 384], P(('groups', 'expert'), 'dp'), parts along dimension 0
The draws below stay inside these ranges and needn't reach their ends.
There are 2 independent parts, one for each index of `groups`. The reference program is written for one: setup_inputs(seed, part) draws one part's arguments, and reference() takes and returns one part's arrays. A program takes and returns all parts, laid end to end along the dimension named above; an argument that names none is the same for every part. Nothing has to cross between parts.
Inputs may be any that keep to these rules, and one draw needn't show every extreme that they name: `routes`: each row names 8 different experts; within each aligned block of 128 rows no expert is named more than 64 times, a bound that some block reaches; every expert is named somewhere.
All inputs are finite; a program needn't handle non-finite values.
Results may differ from the reference program's by a relative error of at most 0.012.
Values may be sent and summed in bfloat16 or wider, within the bound.
No kernel may reach another device: no remote copies, remote signals or barrier semaphores. Data moves between devices by JAX's collectives and lax.ppermute only.
A program may use at most 64 MiB of HBM per device.

```python
import math
import jax
import jax.numpy as jnp
import numpy as np
from jax import lax

D = 1024
FF = 384
TOP = 8
TOK_DEV = 128
EXPERTS = 16
CAP = 64
TOKENS = 2048
N_EXPERT = 16
N_DP = 1


def levels(key, dims, shards, least, high):
    factor_of = 1.0
    for position, blocks in shards:
        heights = jax.random.uniform(jax.random.fold_in(jax.random.fold_in(key, 6), position), (blocks,), jnp.float32, least / len(shards), high / len(shards))
        factor_of = factor_of * jnp.repeat(jnp.exp(heights), dims[position] // blocks).reshape((-1,) + (1,) * (len(dims) - 1 - position))
    return factor_of


def deal_out(own_key, own, number, rows, number_of, top, bound, skew):
    sequence = jax.random.permutation(own_key, number_of)
    packed, ordinary = load_shares(number_of, rows * top, bound, skew, True), load_shares(number_of, rows * top, bound, skew, False)
    places = jnp.arange(number_of)

    def named(tallies, rotation):
        used = int((tallies > 0).sum())
        fixed = max(1, used // 4)
        shifted = fixed + (places - fixed + rotation * (used - fixed)) % max(1, number_of - fixed)
        return jnp.zeros((number_of,), jnp.int32).at[sequence[jnp.where(places < fixed, places, shifted)]].set(jnp.asarray(tallies, jnp.int32))

    tallies = jnp.where(number % 4 == 0, named(packed, number // 4), named(ordinary, number - number // 4 - 1))
    mixed = jax.random.permutation(jax.random.fold_in(own, 3), number_of)
    source_of, taker = mixed[0:number_of // 2 * 2:2], mixed[1:number_of // 2 * 2:2]
    margin = jnp.minimum(tallies[source_of] - 1, bound - tallies[taker]) // 2
    margin = jnp.where((source_of == sequence[0]) | (taker == sequence[0]) | (tallies[taker] == 0), 0, jnp.maximum(margin, 0))
    shifted = jax.random.randint(jax.random.fold_in(own, 4), (number_of // 2,), 0, 1 << 20) % (margin + 1)
    tallies = tallies.at[source_of].add(-shifted).at[taker].add(shifted)
    members = jnp.searchsorted(jnp.cumsum(tallies), jnp.arange(rows * top), side="right").astype(jnp.int32)
    table = members.reshape(top, rows).T
    table = table[jax.random.permutation(jax.random.fold_in(own, 1), rows)]
    rotation = jax.random.randint(jax.random.fold_in(own, 2), (rows, 1), 0, top)
    return jnp.take_along_axis(table, (jnp.arange(top)[None, :] + rotation) % top, axis=1)


def load_shares(count, total, most, skew, full):
    portions = [(1 << 20) // math.isqrt(rank ** skew) + 1 for rank in range(1, count + 1)]
    largest = most if full else min(most, max(-(-total // count), total * portions[0] // sum(portions)))
    least = 1 if total - largest >= count - 1 else 0
    given, spare = [largest] + [least] * (count - 1), total - largest - least * (count - 1)
    while spare > 0:
        free = [i for i in range(1, count) if given[i] < largest] or [i for i in range(1, count) if given[i] < most]
        pool, left = sum([portions[i] for i in free]), spare
        for i in free:
            extra = min(most - given[i], max(1, left * portions[i] // pool), spare)
            given[i] = given[i] + extra
            spare = spare - extra
    return np.array(given)


def scatter_about(rng, shape, width, limit, cuts=(), held_as=jnp.bfloat16):
    result = jax.random.normal(rng, shape, jnp.float32) * width
    if len(cuts) > 0:
        result = levels(rng, shape, cuts, -0.22, 0.18) * result
    return jnp.clip(result, min=-limit, max=limit).astype(held_as)


def setup_inputs(seed: int = 0, part: int = 0) -> dict:
    splits = jax.random.split(jax.random.key(seed), 8)
    part_keys = jax.random.split(jax.random.fold_in(splits[7], part), 8)
    tokens = scatter_about(part_keys[0], (TOKENS, D), 1.0, 6.0, ((0, 16),))
    cotangent = scatter_about(part_keys[1], (TOKENS, D), 1.0, 6.0, ((0, 16),))
    routes_keys = jax.random.split(jax.random.fold_in(part_keys[2], 1), TOKENS // TOK_DEV)
    routes_turns = jax.random.permutation(jax.random.fold_in(part_keys[2], 3), TOKENS // TOK_DEV)
    routes = jax.vmap(lambda own, number: deal_out(jax.random.fold_in(part_keys[2], 2), own, number, TOK_DEV, EXPERTS, TOP, CAP, 2))(routes_keys, routes_turns).reshape((TOKENS, TOP))
    combine = jnp.clip(0.2 + 0.8 * jax.random.uniform(part_keys[3], (TOKENS, TOP), jnp.float32) ** levels(part_keys[3], (TOKENS, TOP), ((0, 16),), -0.2, 0.2), 0.2, 1.0)
    w_gate = scatter_about(splits[4], (EXPERTS, D, FF), D ** -0.5, 0.1875, ((0, 16),))
    w_up = scatter_about(splits[5], (EXPERTS, D, FF), D ** -0.5, 0.1875, ((0, 16),))
    w_down = scatter_about(splits[6], (EXPERTS, D, FF), FF ** -0.5, 0.3125, ((0, 16),))
    return dict(tokens=tokens, cotangent=cotangent, routes=routes, combine=combine, w_gate=w_gate, w_up=w_up, w_down=w_down)


def slots_of(routes):
    blocks = routes.reshape(-1, TOK_DEV * TOP)
    onehot = (blocks[:, :, None] == jnp.arange(EXPERTS, dtype=jnp.int32)[None, None, :]).astype(jnp.int32)
    rank = jnp.cumsum(onehot, axis=1) - onehot
    return jnp.sum(rank * onehot, axis=2).astype(jnp.int32)


def contract_last(left, right):
    return lax.dot_general(left, right, (((1,), (1,)), ((), ())), preferred_element_type=jnp.float32)


def reference(tokens, cotangent, routes, combine, w_gate, w_up, w_down):
    nblocks = TOKENS // TOK_DEV
    slot = slots_of(routes).reshape(-1)
    expert_id = routes.reshape(-1).astype(jnp.int32)
    token_id = jnp.repeat(jnp.arange(TOKENS, dtype=jnp.int32), TOP)
    block_id = (token_id // TOK_DEV).astype(jnp.int32)
    table = jnp.full((EXPERTS, nblocks, CAP), TOKENS, jnp.int32).at[expert_id, block_id, slot].set(token_id)
    scales = jnp.zeros((EXPERTS, nblocks, CAP), jnp.float32).at[expert_id, block_id, slot].set(combine.reshape(-1).astype(jnp.float32))

    def split(matrix):
        return matrix.reshape(N_EXPERT, N_DP, CAP, -1).astype(jnp.float32)

    def partial_sum(left, right):
        terms = jnp.einsum('ipcd,ipcf->pdf', split(left), split(right), precision=lax.Precision.HIGHEST)
        return jnp.sum(terms.astype(jnp.bfloat16).astype(jnp.float32), axis=0).astype(jnp.bfloat16)

    def expert_step(carry, item):
        mixed_sum, grad_sum = carry
        index, scale, gate_w, up_w, down_w = item
        flat = index.reshape(-1)
        valid = flat < TOKENS
        safe = jnp.minimum(flat, TOKENS - 1)
        weight = scale.reshape(-1)
        rows = jnp.where(valid[:, None], tokens[safe], jnp.zeros((), jnp.bfloat16))
        gate = jnp.dot(rows, gate_w, preferred_element_type=jnp.float32)
        up = jnp.dot(rows, up_w, preferred_element_type=jnp.float32)
        sig = jax.nn.sigmoid(gate)
        act = gate * sig
        hidden = (act * up).astype(jnp.bfloat16)
        produced = contract_last(hidden, down_w).astype(jnp.bfloat16)
        mixed_sum = mixed_sum.at[flat].add(weight[:, None] * produced.astype(jnp.float32), mode="drop")
        grad_rows = jnp.where(valid[:, None], weight[:, None] * cotangent[safe].astype(jnp.float32), jnp.zeros((), jnp.float32)).astype(jnp.bfloat16)
        dhidden = jnp.dot(grad_rows, down_w, preferred_element_type=jnp.float32)
        dgate = (dhidden * up * sig * (1.0 + gate * (1.0 - sig))).astype(jnp.bfloat16)
        dup = (dhidden * act).astype(jnp.bfloat16)
        dinput = (contract_last(dgate, gate_w) + contract_last(dup, up_w)).astype(jnp.bfloat16)
        grad_sum = grad_sum.at[flat].add(dinput.astype(jnp.float32), mode="drop")
        grads = (partial_sum(rows, dgate), partial_sum(rows, dup), partial_sum(grad_rows, hidden))
        return (mixed_sum, grad_sum), grads

    start = (jnp.zeros((TOKENS, D), jnp.float32), jnp.zeros((TOKENS, D), jnp.float32))
    (mixed_sum, grad_sum), grads = lax.scan(expert_step, start, (table, scales, w_gate, w_up, w_down))
    return (mixed_sum.astype(jnp.bfloat16), grad_sum.astype(jnp.bfloat16), grads[0], grads[1], grads[2])
```

```python
import functools

import jax
import jax.numpy as jnp
from jax import lax
from jax.experimental import pallas as pl
from jax.experimental.pallas import tpu as pltpu
from jax.sharding import PartitionSpec as P

F32 = jnp.float32
BF16 = jnp.bfloat16


def contract_last(left, right):
    return lax.dot_general(
        left, right, (((1,), (1,)), ((), ())), preferred_element_type=jnp.float32
    )


def contract_first(left, right):
    return lax.dot_general(
        left, right, (((0,), (0,)), ((), ())), preferred_element_type=jnp.float32
    )


def by_all_to_all(tokens, cotangent, routes, combine, w_gate, w_up, w_down):
    tok_dev, width = tokens.shape
    top_count = routes.shape[1]
    experts = w_gate.shape[0] * lax.axis_size("expert")
    capacity = min(tok_dev, max(2, (tok_dev * top_count + experts - 1) // experts))
    flat = routes.reshape(-1)
    onehot = (flat[:, None] == jnp.arange(experts, dtype=jnp.int32)[None, :]).astype(jnp.int32)
    rank = jnp.cumsum(onehot, axis=0) - onehot
    place = flat * capacity + jnp.sum(rank * onehot, axis=1)
    owner = jnp.arange(tok_dev * top_count, dtype=jnp.int32) // top_count

    def fill_slots(values):
        empty = jnp.zeros((experts * capacity, width), jnp.bfloat16)
        return empty.at[place].set(values).reshape(experts, capacity, width)

    def collect(returned):
        picked = returned.reshape(-1, width)[place].astype(jnp.float32)
        return picked.reshape(tok_dev, top_count, width)

    outgoing = fill_slots(tokens[owner])
    weighted = (combine.reshape(-1)[:, None] * cotangent[owner].astype(jnp.float32)).astype(
        jnp.bfloat16
    )
    arrived = lax.all_to_all(outgoing, "expert", split_axis=0, concat_axis=0, tiled=True)
    rows = arrived.reshape(-1, width)
    gate_w = w_gate[0]
    up_w = w_up[0]
    down_w = w_down[0]
    gate = jnp.dot(rows, gate_w, preferred_element_type=jnp.float32)
    up = jnp.dot(rows, up_w, preferred_element_type=jnp.float32)
    sig = jax.nn.sigmoid(gate)
    act = gate * sig
    hidden = (act * up).astype(jnp.bfloat16)
    produced = contract_last(hidden, down_w).astype(jnp.bfloat16).reshape(arrived.shape)
    returned = lax.all_to_all(produced, "expert", split_axis=0, concat_axis=0, tiled=True)
    mixed = jnp.sum(collect(returned) * combine[:, :, None], axis=1).astype(jnp.bfloat16)
    grad_arrived = lax.all_to_all(
        fill_slots(weighted), "expert", split_axis=0, concat_axis=0, tiled=True
    )
    grad_rows = grad_arrived.reshape(-1, width)
    dhidden = jnp.dot(grad_rows, down_w, preferred_element_type=jnp.float32)
    dgate = (dhidden * up * sig * (1.0 + gate * (1.0 - sig))).astype(jnp.bfloat16)
    dup = (dhidden * act).astype(jnp.bfloat16)
    dinput = (contract_last(dgate, gate_w) + contract_last(dup, up_w)).astype(jnp.bfloat16)
    back = lax.all_to_all(
        dinput.reshape(arrived.shape), "expert", split_axis=0, concat_axis=0, tiled=True
    )
    grad_tokens = jnp.sum(collect(back), axis=1).astype(jnp.bfloat16)
    summed = lax.psum_scatter(
        jnp.concatenate(
            [
                contract_first(rows, dgate),
                contract_first(rows, dup),
                contract_first(grad_rows, hidden),
            ],
            axis=1,
        ).astype(jnp.bfloat16),
        "dp",
        scatter_dimension=0,
        tiled=True,
    ).astype(jnp.float32)
    hidden_units = gate_w.shape[1]
    grad_gate = summed[:, :hidden_units].astype(jnp.bfloat16)[None]
    grad_up = summed[:, hidden_units : 2 * hidden_units].astype(jnp.bfloat16)[None]
    grad_down = summed[:, 2 * hidden_units :].astype(jnp.bfloat16)[None]
    return (mixed, grad_tokens, grad_gate, grad_up, grad_down)


VMEM = pltpu.VMEM
LIMIT = 20 * 1024 * 1024


def call(body, outs, operands, flops, smem=0, scratch=(), nbytes=None):
    specs = [pl.BlockSpec(memory_space=pltpu.SMEM)] * smem
    specs += [pl.BlockSpec(memory_space=VMEM)] * (len(operands) - smem)
    if nbytes is None:
        nbytes = sum(a.size * a.dtype.itemsize for a in operands)
        nbytes += sum(a.size * a.dtype.itemsize for a in outs)
    return pl.pallas_call(
        body,
        out_shape=list(outs),
        in_specs=specs,
        out_specs=[pl.BlockSpec(memory_space=VMEM)] * len(outs),
        scratch_shapes=list(scratch),
        compiler_params=pltpu.CompilerParams(vmem_limit_bytes=LIMIT),
        cost_estimate=pl.CostEstimate(flops=flops, bytes_accessed=nbytes, transcendentals=0),
    )(*operands)


def picks(place, cap):
    slots = lax.broadcasted_iota(jnp.int32, (cap, place.shape[1]), 0).astype(F32)
    return jnp.where(slots == place, 1.0, 0.0)


def joined(parts):
    return parts[0] if len(parts) == 1 else jnp.concatenate(parts, axis=0)


def forward_body(dirs, halves, cap, top, expert_ref, *refs):
    metas = refs[:dirs]
    refs = refs[dirs:]
    count = dirs * halves
    own = refs[:count]
    other = refs[count : 2 * count]
    w_gate, w_up, w_down = refs[2 * count : 2 * count + 3]
    info_ref, rows_ref, slope_ref, act_ref, hidden_ref, keep_ref, give_ref = refs[2 * count + 3 :]
    me = expert_ref[0].astype(F32)
    mate = expert_ref[1].astype(F32)
    tok = metas[0].shape[1]
    masks, weights = [], []
    for expert, side in ((me, 0), (me, 1), (mate, 0)):
        for d in range(dirs):
            base = side * 2 * top
            hit = metas[d][base : base + top] == expert
            masks.append(jnp.sum(jnp.where(hit, 1.0, 0.0), axis=0, keepdims=True))
            share = jnp.where(hit, metas[d][base + top : base + 2 * top], 0.0)
            weights.append(jnp.sum(share, axis=0, keepdims=True))
    pad = jnp.zeros((8 - len(masks), tok), F32)
    mask = jnp.concatenate(masks + [pad], axis=0)
    before = lax.broadcasted_iota(jnp.int32, (tok, tok), 0) < lax.broadcasted_iota(
        jnp.int32, (tok, tok), 1
    )
    rank = jnp.dot(
        mask.astype(BF16), jnp.where(before, 1.0, 0.0).astype(BF16), preferred_element_type=F32
    )
    place = jnp.where(mask > 0.5, rank, -1.0)
    info_ref[0:8] = place
    info_ref[8:16] = jnp.concatenate(weights + [pad], axis=0)
    share = []
    for side, blocks in enumerate((own, other)):
        for d in range(dirs):
            i = side * dirs + d
            pick = picks(place[i : i + 1], cap)
            share.append(jnp.sum(pick * weights[i], axis=1, keepdims=True))
            block = joined([b[...] for b in blocks[d * halves : (d + 1) * halves]])
            taken = jnp.dot(pick.astype(BF16), block, preferred_element_type=F32)
            rows_ref[i * cap : (i + 1) * cap] = taken.astype(BF16)
    rows = rows_ref[...]
    gate = jnp.dot(rows, w_gate[...], preferred_element_type=F32)
    up = jnp.dot(rows, w_up[...], preferred_element_type=F32)
    sig = jax.nn.sigmoid(gate)
    act = gate * sig
    hidden = (act * up).astype(BF16)
    hidden_ref[...] = hidden
    act_ref[...] = act
    slope_ref[...] = up * sig * (1.0 + gate * (1.0 - sig))
    produced = contract_last(hidden, w_down[...]).astype(BF16).astype(F32)
    sent = (jnp.concatenate(share, axis=0) * produced).astype(BF16)
    keep_ref[...] = sent[: dirs * cap]
    give_ref[...] = sent[dirs * cap :]


def backward_body(dirs, halves, cap, *refs):
    count = dirs * halves
    info_ref, slope, act = refs[:3]
    own = refs[3 : 3 + count]
    other = refs[3 + count : 3 + 2 * count]
    w_gate, w_up, w_down = refs[3 + 2 * count : 6 + 2 * count]
    rows_ref, dgate_ref, dup_ref, keep_ref, give_ref = refs[6 + 2 * count :]
    for side, blocks in enumerate((own, other)):
        for d in range(dirs):
            i = side * dirs + d
            pick = picks(info_ref[i : i + 1], cap)
            share = jnp.sum(pick * info_ref[8 + i : 9 + i], axis=1, keepdims=True)
            block = joined([b[...] for b in blocks[d * halves : (d + 1) * halves]])
            taken = jnp.dot(pick.astype(BF16), block, preferred_element_type=F32)
            rows_ref[i * cap : (i + 1) * cap] = (share * taken).astype(BF16)
    dhidden = jnp.dot(rows_ref[...], w_down[...], preferred_element_type=F32)
    dgate = (dhidden * slope[...]).astype(BF16)
    dup = (dhidden * act[...]).astype(BF16)
    dgate_ref[...] = dgate
    dup_ref[...] = dup
    back = (contract_last(dgate, w_gate[...]) + contract_last(dup, w_up[...])).astype(BF16)
    keep_ref[...] = back[: dirs * cap]
    give_ref[...] = back[dirs * cap :]


def return_body(dirs, cap, arrived, info_ref, keep, give, *refs):
    ins = refs[: len(arrived)]
    outs = refs[len(arrived) :]
    sums = []
    for d in range(dirs):
        both = jnp.concatenate(
            [picks(info_ref[d : d + 1], cap), picks(info_ref[2 * dirs + d : 2 * dirs + d + 1], cap)],
            axis=0,
        ).astype(BF16)
        part = slice(d * cap, (d + 1) * cap)
        values = jnp.concatenate([keep[part], give[part]], axis=0)
        sums.append(contract_first(both, values))
    if dirs == 1 and len(outs) == 2:
        half = sums[0].shape[0] // 2
        outs[0][...] = sums[0][:half].astype(BF16)
        outs[1][...] = sums[0][half:].astype(BF16)
        return
    for d in range(dirs):
        total = sums[d]
        for ref, (which, low, high) in zip(ins, arrived):
            if which != d:
                continue
            value = ref[...].astype(F32)
            tok = total.shape[0]
            if high - low == tok:
                total = total + value
            else:
                pieces = []
                if low:
                    pieces.append(total[:low])
                pieces.append(total[low:high] + value)
                if high < tok:
                    pieces.append(total[high:])
                total = jnp.concatenate(pieces, axis=0)
        outs[d][...] = total.astype(BF16)


def weights_body(steps, cols, *refs):
    rows = refs[:steps]
    grads = refs[steps : 2 * steps]
    out = refs[2 * steps]
    right = jnp.concatenate([g[...] for g in grads], axis=0)
    for low in range(0, out.shape[0], cols):
        left = jnp.concatenate([r[:, low : low + cols] for r in rows], axis=0)
        out[low : low + cols] = contract_first(left, right).astype(BF16)


def by_ring(tokens, cotangent, routes, combine, w_gate, w_up, w_down):
    tok, width = tokens.shape
    top = routes.shape[1]
    n = lax.axis_size("expert")
    cap = (tok * top + n - 1) // n
    units = w_gate.shape[2]
    gate_w, up_w, down_w = w_gate[0], w_up[0], w_down[0]
    pairs = n // 2
    reach = pairs // 2
    half = tok // 2
    walk = [2 * i for i in range(reach)] + [2 * i + 1 for i in reversed(range(reach))]

    def hop(value, by):
        moves = [
            (2 * walk[i] + core, 2 * walk[(i + by) % pairs] + core)
            for i in range(pairs)
            for core in range(2)
        ]
        return lax.ppermute(value, "expert", moves)

    def swap(value):
        return lax.ppermute(value, "expert", [(i, i ^ 1) for i in range(n)])

    def spread(block, split):
        found = [[block]]
        back = front = block
        for step in range(1, reach + 1):
            if step == reach and split:
                back, front = hop(back[:half], 1), hop(front[half:], -1)
            elif step == reach:
                found.append([hop(back, 1)])
                break
            else:
                back, front = hop(back, 1), hop(front, -1)
            found.append([back, front])
        return found

    here = lax.axis_index("expert").astype(jnp.int32)
    expert = jnp.stack([here, here ^ 1])
    meta = jnp.concatenate([routes.T.astype(F32), combine.T], axis=0)
    metas = spread(jnp.concatenate([meta, swap(meta)], axis=0), False)
    token_blocks = spread(tokens, True)
    token_other = [[swap(b) for b in found] for found in token_blocks]
    cot_blocks = spread(cotangent, True)
    cot_other = [[swap(b) for b in found] for found in cot_blocks]

    def struct(shape, dtype):
        return jax.ShapeDtypeStruct(shape, dtype)

    forward, backward = [], []
    for step in range(reach + 1):
        dirs = 2 if 0 < step < reach else 1
        halves = 2 if step == reach else 1
        m = 2 * dirs * cap
        forward.append(
            call(
                functools.partial(forward_body, dirs, halves, cap, top),
                [
                    struct((16, tok), F32),
                    struct((m, width), BF16),
                    struct((m, units), F32),
                    struct((m, units), F32),
                    struct((m, units), BF16),
                    struct((m // 2, width), BF16),
                    struct((m // 2, width), BF16),
                ],
                [expert, *metas[step], *token_blocks[step], *token_other[step], gate_w, up_w, down_w],
                2 * m * width * (3 * units + tok),
                smem=1,
            )
        )
    for step in range(reach + 1):
        dirs = 2 if 0 < step < reach else 1
        halves = 2 if step == reach else 1
        m = 2 * dirs * cap
        info, _, slope, act = forward[step][:4]
        backward.append(
            call(
                functools.partial(backward_body, dirs, halves, cap),
                [
                    struct((m, width), BF16),
                    struct((m, units), BF16),
                    struct((m, units), BF16),
                    struct((m // 2, width), BF16),
                    struct((m // 2, width), BF16),
                ],
                [info, slope, act, *cot_blocks[step], *cot_other[step], gate_w, up_w, down_w],
                2 * m * width * (3 * units + tok),
            )
        )

    def gather_sums(kept, given):
        given = [swap(g) for g in given]
        flops = 4 * cap * tok * width

        def stage(step, arrived, values, outs):
            dirs = 2 if 0 < step < reach else 1
            return call(
                functools.partial(return_body, dirs, cap, arrived),
                [struct((rows, width), BF16) for rows in outs],
                [forward[step][0], kept[step], given[step], *values],
                dirs * flops,
            )

        ahead, behind = stage(reach, (), (), (half, half))
        ahead, behind = hop(ahead, 1), hop(behind, -1)
        for step in range(reach - 1, 0, -1):
            first = step == reach - 1
            arrived = (
                (0, half if first else 0, tok),
                (1, 0, half if first else tok),
            )
            behind, ahead = stage(step, arrived, (behind, ahead), (tok, tok))
            ahead, behind = hop(ahead, 1), hop(behind, -1)
        alone = reach == 1
        arrived = ((0, 0, half if alone else tok), (0, half if alone else 0, tok))
        return stage(0, arrived, (ahead, behind), (tok,))[0]

    mixed = gather_sums([f[5] for f in forward], [f[6] for f in forward])
    grad_tokens = gather_sums([b[3] for b in backward], [b[4] for b in backward])

    def weight_grad(lefts, rights):
        return call(
            functools.partial(weights_body, len(lefts), 256),
            [struct((width, units), BF16)],
            [*lefts, *rights],
            2 * n * cap * width * units,
        )[0][None]

    grad_gate = weight_grad([f[1] for f in forward], [b[1] for b in backward])
    grad_up = weight_grad([f[1] for f in forward], [b[2] for b in backward])
    grad_down = weight_grad([b[0] for b in backward], [f[4] for f in forward])
    return (mixed, grad_tokens, grad_gate, grad_up, grad_down)


def per_device(tokens, cotangent, routes, combine, w_gate, w_up, w_down):
    n = lax.axis_size("expert")
    tok, width = tokens.shape
    top = routes.shape[1]
    ring = (
        lax.axis_size("dp") == 1
        and w_gate.shape[0] == 1
        and n % 4 == 0
        and n <= 2 * top
        and tok % 128 == 0
        and top % 8 == 0
        and (tok * top) % (16 * n) == 0
    )
    plan = by_ring if ring else by_all_to_all
    return plan(tokens, cotangent, routes, combine, w_gate, w_up, w_down)


def solution(mesh):
    placed = (
        P(("groups", "expert", "dp"), None),
        P(("groups", "expert", "dp"), None),
        P(("groups", "expert", "dp"), None),
        P(("groups", "expert", "dp"), None),
        P("expert", None, None),
        P("expert", None, None),
        P("expert", None, None),
    )
    return jax.shard_map(
        per_device,
        mesh=mesh,
        in_specs=placed,
        out_specs=(
            P(("groups", "expert", "dp"), None),
            P(("groups", "expert", "dp"), None),
            P(("groups", "expert"), "dp", None),
            P(("groups", "expert"), "dp", None),
            P(("groups", "expert"), "dp", None),
        ),
        check_vma=False,
    )
```

```python
import functools

import jax
import jax.numpy as jnp
from jax import lax
from jax.experimental import pallas as pl
from jax.experimental.pallas import tpu as pltpu
from jax.sharding import PartitionSpec as P

F32 = jnp.float32
BF16 = jnp.bfloat16


def contract_last(left, right):
    return lax.dot_general(
        left, right, (((1,), (1,)), ((), ())), preferred_element_type=jnp.float32
    )


def contract_first(left, right):
    return lax.dot_general(
        left, right, (((0,), (0,)), ((), ())), preferred_element_type=jnp.float32
    )


def by_all_to_all(tokens, cotangent, routes, combine, w_gate, w_up, w_down):
    tok_dev, width = tokens.shape
    top_count = routes.shape[1]
    experts = w_gate.shape[0] * lax.axis_size("expert")
    capacity = min(tok_dev, max(2, (tok_dev * top_count + experts - 1) // experts))
    flat = routes.reshape(-1)
    onehot = (flat[:, None] == jnp.arange(experts, dtype=jnp.int32)[None, :]).astype(jnp.int32)
    rank = jnp.cumsum(onehot, axis=0) - onehot
    place = flat * capacity + jnp.sum(rank * onehot, axis=1)
    owner = jnp.arange(tok_dev * top_count, dtype=jnp.int32) // top_count

    def fill_slots(values):
        empty = jnp.zeros((experts * capacity, width), jnp.bfloat16)
        return empty.at[place].set(values).reshape(experts, capacity, width)

    def collect(returned):
        picked = returned.reshape(-1, width)[place].astype(jnp.float32)
        return picked.reshape(tok_dev, top_count, width)

    outgoing = fill_slots(tokens[owner])
    weighted = (combine.reshape(-1)[:, None] * cotangent[owner].astype(jnp.float32)).astype(
        jnp.bfloat16
    )
    arrived = lax.all_to_all(outgoing, "expert", split_axis=0, concat_axis=0, tiled=True)
    rows = arrived.reshape(-1, width)
    gate_w = w_gate[0]
    up_w = w_up[0]
    down_w = w_down[0]
    gate = jnp.dot(rows, gate_w, preferred_element_type=jnp.float32)
    up = jnp.dot(rows, up_w, preferred_element_type=jnp.float32)
    sig = jax.nn.sigmoid(gate)
    act = gate * sig
    hidden = (act * up).astype(jnp.bfloat16)
    produced = contract_last(hidden, down_w).astype(jnp.bfloat16).reshape(arrived.shape)
    returned = lax.all_to_all(produced, "expert", split_axis=0, concat_axis=0, tiled=True)
    mixed = jnp.sum(collect(returned) * combine[:, :, None], axis=1).astype(jnp.bfloat16)
    grad_arrived = lax.all_to_all(
        fill_slots(weighted), "expert", split_axis=0, concat_axis=0, tiled=True
    )
    grad_rows = grad_arrived.reshape(-1, width)
    dhidden = jnp.dot(grad_rows, down_w, preferred_element_type=jnp.float32)
    dgate = (dhidden * up * sig * (1.0 + gate * (1.0 - sig))).astype(jnp.bfloat16)
    dup = (dhidden * act).astype(jnp.bfloat16)
    dinput = (contract_last(dgate, gate_w) + contract_last(dup, up_w)).astype(jnp.bfloat16)
    back = lax.all_to_all(
        dinput.reshape(arrived.shape), "expert", split_axis=0, concat_axis=0, tiled=True
    )
    grad_tokens = jnp.sum(collect(back), axis=1).astype(jnp.bfloat16)
    summed = lax.psum_scatter(
        jnp.concatenate(
            [
                contract_first(rows, dgate),
                contract_first(rows, dup),
                contract_first(grad_rows, hidden),
            ],
            axis=1,
        ).astype(jnp.bfloat16),
        "dp",
        scatter_dimension=0,
        tiled=True,
    ).astype(jnp.float32)
    hidden_units = gate_w.shape[1]
    grad_gate = summed[:, :hidden_units].astype(jnp.bfloat16)[None]
    grad_up = summed[:, hidden_units : 2 * hidden_units].astype(jnp.bfloat16)[None]
    grad_down = summed[:, 2 * hidden_units :].astype(jnp.bfloat16)[None]
    return (mixed, grad_tokens, grad_gate, grad_up, grad_down)


VMEM = pltpu.VMEM
LIMIT = 20 * 1024 * 1024


def call(body, outs, operands, flops, smem=0, scratch=(), nbytes=None):
    specs = [pl.BlockSpec(memory_space=pltpu.SMEM)] * smem
    specs += [pl.BlockSpec(memory_space=VMEM)] * (len(operands) - smem)
    if nbytes is None:
        nbytes = sum(a.size * a.dtype.itemsize for a in operands)
        nbytes += sum(a.size * a.dtype.itemsize for a in outs)
    return pl.pallas_call(
        body,
        out_shape=list(outs),
        in_specs=specs,
        out_specs=[pl.BlockSpec(memory_space=VMEM)] * len(outs),
        scratch_shapes=list(scratch),
        compiler_params=pltpu.CompilerParams(vmem_limit_bytes=LIMIT),
        cost_estimate=pl.CostEstimate(flops=flops, bytes_accessed=nbytes, transcendentals=0),
    )(*operands)


def picks(place, cap):
    slots = lax.broadcasted_iota(jnp.int32, (cap, place.shape[1]), 0).astype(F32)
    return jnp.where(slots == place, 1.0, 0.0)


def joined(parts):
    return parts[0] if len(parts) == 1 else jnp.concatenate(parts, axis=0)


def payload_body(routes_ref, combine_ref, tokens_ref, out_ref):
    top, tok = routes_ref.shape
    exact = combine_ref[...]
    high = exact.astype(BF16)
    rest = exact - high.astype(F32)
    middle = rest.astype(BF16)
    low = (rest - middle.astype(F32)).astype(BF16)
    blank = jnp.zeros((top, tok), F32)
    names = jnp.concatenate([routes_ref[...].astype(F32), high.astype(F32)], axis=0)
    out_ref[: 2 * top] = jnp.zeros((2 * top, out_ref.shape[1]), BF16)
    out_ref[: 2 * top, :tok] = names.astype(BF16)
    for i, term in enumerate((middle, low)):
        padded = jnp.concatenate([blank, term.astype(F32)], axis=0)
        out_ref[: 2 * top, (i + 1) * tok : (i + 2) * tok] = padded.astype(BF16)
    out_ref[2 * top :] = tokens_ref[...]


def forward_body(dirs, halves, cap, top, expert_ref, *refs):
    count = dirs * halves
    sides = (refs[:count], refs[count : 2 * count])
    w_gate, w_up, w_down = refs[2 * count : 2 * count + 3]
    info_ref, rows_ref, slope_ref, act_ref, hidden_ref, keep_ref, give_ref = refs[2 * count + 3 :]
    me = expert_ref[0].astype(F32)
    mate = expert_ref[1].astype(F32)
    head = 2 * top
    tok = info_ref.shape[1]
    names, terms = [], []
    for blocks in sides:
        for d in range(dirs):
            told = blocks[d * halves][:head, : 3 * tok].astype(F32)
            names.append(told[:top, :tok])
            told = told[top:]
            terms.append(told[:, :tok] + (told[:, tok : 2 * tok] + told[:, 2 * tok :]))
    masks, weights = [], []
    for expert, which in [(me, i) for i in range(2 * dirs)] + [(mate, i) for i in range(dirs)]:
        hit = names[which] == expert
        masks.append(jnp.sum(jnp.where(hit, 1.0, 0.0), axis=0, keepdims=True))
        weights.append(jnp.sum(jnp.where(hit, terms[which], 0.0), axis=0, keepdims=True))
    pad = jnp.zeros((8 - len(masks), tok), F32)
    mask = jnp.concatenate(masks + [pad], axis=0)
    before = lax.broadcasted_iota(jnp.int32, (tok, tok), 0) < lax.broadcasted_iota(
        jnp.int32, (tok, tok), 1
    )
    rank = jnp.dot(
        mask.astype(BF16), jnp.where(before, 1.0, 0.0).astype(BF16), preferred_element_type=F32
    )
    place = jnp.where(mask > 0.5, rank, -1.0)
    info_ref[0:8] = place
    info_ref[8:16] = jnp.concatenate(weights + [pad], axis=0)
    share = []
    for side, blocks in enumerate(sides):
        for d in range(dirs):
            i = side * dirs + d
            pick = picks(place[i : i + 1], cap)
            share.append(jnp.sum(pick * weights[i], axis=1, keepdims=True))
            first, *others = blocks[d * halves : (d + 1) * halves]
            block = joined([first[head:]] + [b[...] for b in others])
            taken = jnp.dot(pick.astype(BF16), block, preferred_element_type=F32)
            rows_ref[i * cap : (i + 1) * cap] = taken.astype(BF16)
    rows = rows_ref[...]
    gate = jnp.dot(rows, w_gate[...], preferred_element_type=F32)
    up = jnp.dot(rows, w_up[...], preferred_element_type=F32)
    sig = jax.nn.sigmoid(gate)
    act = gate * sig
    hidden = (act * up).astype(BF16)
    hidden_ref[...] = hidden
    act_ref[...] = act
    slope_ref[...] = up * sig * (1.0 + gate * (1.0 - sig))
    produced = contract_last(hidden, w_down[...]).astype(BF16).astype(F32)
    sent = (jnp.concatenate(share, axis=0) * produced).astype(BF16)
    keep_ref[...] = sent[: dirs * cap]
    give_ref[...] = sent[dirs * cap :]


def backward_body(dirs, halves, cap, *refs):
    count = dirs * halves
    info_ref, slope, act = refs[:3]
    own = refs[3 : 3 + count]
    other = refs[3 + count : 3 + 2 * count]
    w_gate, w_up, w_down = refs[3 + 2 * count : 6 + 2 * count]
    rows_ref, dgate_ref, dup_ref, keep_ref, give_ref = refs[6 + 2 * count :]
    for side, blocks in enumerate((own, other)):
        for d in range(dirs):
            i = side * dirs + d
            pick = picks(info_ref[i : i + 1], cap)
            share = jnp.sum(pick * info_ref[8 + i : 9 + i], axis=1, keepdims=True)
            block = joined([b[...] for b in blocks[d * halves : (d + 1) * halves]])
            taken = jnp.dot(pick.astype(BF16), block, preferred_element_type=F32)
            rows_ref[i * cap : (i + 1) * cap] = (share * taken).astype(BF16)
    dhidden = jnp.dot(rows_ref[...], w_down[...], preferred_element_type=F32)
    dgate = (dhidden * slope[...]).astype(BF16)
    dup = (dhidden * act[...]).astype(BF16)
    dgate_ref[...] = dgate
    dup_ref[...] = dup
    back = (contract_last(dgate, w_gate[...]) + contract_last(dup, w_up[...])).astype(BF16)
    keep_ref[...] = back[: dirs * cap]
    give_ref[...] = back[dirs * cap :]


def return_body(dirs, cap, arrived, info_ref, keep, give, *refs):
    ins = refs[: len(arrived)]
    outs = refs[len(arrived) :]
    sums = []
    for d in range(dirs):
        both = jnp.concatenate(
            [picks(info_ref[d : d + 1], cap), picks(info_ref[2 * dirs + d : 2 * dirs + d + 1], cap)],
            axis=0,
        ).astype(BF16)
        part = slice(d * cap, (d + 1) * cap)
        values = jnp.concatenate([keep[part], give[part]], axis=0)
        sums.append(contract_first(both, values))
    if dirs == 1 and len(outs) == 2:
        half = sums[0].shape[0] // 2
        outs[0][...] = sums[0][:half].astype(BF16)
        outs[1][...] = sums[0][half:].astype(BF16)
        return
    for d in range(dirs):
        total = sums[d]
        for ref, (which, low, high) in zip(ins, arrived):
            if which != d:
                continue
            value = ref[...].astype(F32)
            tok = total.shape[0]
            if high - low == tok:
                total = total + value
            else:
                pieces = []
                if low:
                    pieces.append(total[:low])
                pieces.append(total[low:high] + value)
                if high < tok:
                    pieces.append(total[high:])
                total = jnp.concatenate(pieces, axis=0)
        outs[d][...] = total.astype(BF16)


def weights_body(steps, cols, *refs):
    rows = refs[:steps]
    grads = refs[steps : 2 * steps]
    out = refs[2 * steps]
    right = jnp.concatenate([g[...] for g in grads], axis=0)
    for low in range(0, out.shape[0], cols):
        left = jnp.concatenate([r[:, low : low + cols] for r in rows], axis=0)
        out[low : low + cols] = contract_first(left, right).astype(BF16)


def by_ring(tokens, cotangent, routes, combine, w_gate, w_up, w_down):
    tok, width = tokens.shape
    top = routes.shape[1]
    n = lax.axis_size("expert")
    cap = (tok * top + n - 1) // n
    units = w_gate.shape[2]
    gate_w, up_w, down_w = w_gate[0], w_up[0], w_down[0]
    pairs = n // 2
    reach = pairs // 2
    half = tok // 2
    walk = [2 * i for i in range(reach)] + [2 * i + 1 for i in reversed(range(reach))]

    def hop(value, by):
        moves = [
            (2 * walk[i] + core, 2 * walk[(i + by) % pairs] + core)
            for i in range(pairs)
            for core in range(2)
        ]
        return lax.ppermute(value, "expert", moves)

    def after(value, *others):
        return lax.optimization_barrier((value, *others))[0] if others else value

    def swap(value):
        return lax.ppermute(value, "expert", [(i, i ^ 1) for i in range(n)])

    def struct(shape, dtype):
        return jax.ShapeDtypeStruct(shape, dtype)

    def shape_of(step):
        return (2 if 0 < step < reach else 1), (2 if step == reach else 1)

    here = lax.axis_index("expert").astype(jnp.int32)
    expert = jnp.stack([here, here ^ 1])
    head = 2 * top

    def onward(found, step, cut, waits):
        back, front = found[0], found[-1]
        if step == reach:
            back, front = back[: half + cut], front[half + cut :]
        return [hop(after(back, *waits), 1), hop(after(front, *waits), -1)]

    def run_forward(step):
        dirs, halves = shape_of(step)
        m = 2 * dirs * cap
        return call(
            functools.partial(forward_body, dirs, halves, cap, top),
            [
                struct((16, tok), F32),
                struct((m, width), BF16),
                struct((m, units), F32),
                struct((m, units), F32),
                struct((m, units), BF16),
                struct((m // 2, width), BF16),
                struct((m // 2, width), BF16),
            ],
            [expert, *token_own[step], *token_other[step], gate_w, up_w, down_w],
            2 * m * width * (3 * units + tok),
            smem=1,
        )

    def run_backward(step):
        dirs, halves = shape_of(step)
        m = 2 * dirs * cap
        info, _, slope, act = forward[step][:4]
        return call(
            functools.partial(backward_body, dirs, halves, cap),
            [
                struct((m, width), BF16),
                struct((m, units), BF16),
                struct((m, units), BF16),
                struct((m // 2, width), BF16),
                struct((m // 2, width), BF16),
            ],
            [info, slope, act, *cot_own[step], *cot_other[step], gate_w, up_w, down_w],
            2 * m * width * (3 * units + tok),
        )

    payload = call(
        payload_body, [struct((head + tok, width), BF16)], [routes.T, combine.T, tokens], 0
    )[0]
    token_own, cot_own = [[payload]], [[cotangent]]
    token_other, cot_other = [[swap(payload)]], []
    forward, backward = [], []
    for step in range(1, reach + 1):
        waits = [forward[step - 2][0]] if step > 1 else []
        token_own.append(onward(token_own[-1], step, head, waits))
        waits = [token_own[step][0]]
        if step > 1:
            waits.append(backward[step - 2][1])
        token_other.append([swap(b) for b in token_own[step]])
        if step == 1:
            cot_other.append([swap(cotangent)])
        cot_own.append(onward(cot_own[-1], step, 0, waits))
        cot_other.append([swap(b) for b in cot_own[step]])
        forward.append(run_forward(step - 1))
        backward.append(run_backward(step - 1))
    forward.append(run_forward(reach))
    backward.append(run_backward(reach))

    def gather_sums(kept, given):
        given = [swap(g) for g in given]
        flops = 4 * cap * tok * width

        def stage(step, arrived, values, outs):
            dirs = 2 if 0 < step < reach else 1
            return call(
                functools.partial(return_body, dirs, cap, arrived),
                [struct((rows, width), BF16) for rows in outs],
                [forward[step][0], kept[step], given[step], *values],
                dirs * flops,
            )

        ahead, behind = stage(reach, (), (), (half, half))
        ahead, behind = hop(ahead, 1), hop(behind, -1)
        for step in range(reach - 1, 0, -1):
            first = step == reach - 1
            arrived = (
                (0, half if first else 0, tok),
                (1, 0, half if first else tok),
            )
            behind, ahead = stage(step, arrived, (behind, ahead), (tok, tok))
            ahead, behind = hop(ahead, 1), hop(behind, -1)
        alone = reach == 1
        arrived = ((0, 0, half if alone else tok), (0, half if alone else 0, tok))
        return stage(0, arrived, (ahead, behind), (tok,))[0]

    mixed = gather_sums([f[5] for f in forward], [f[6] for f in forward])
    grad_tokens = gather_sums([b[3] for b in backward], [b[4] for b in backward])

    def weight_grad(lefts, rights):
        return call(
            functools.partial(weights_body, len(lefts), 256),
            [struct((width, units), BF16)],
            [*lefts, *rights],
            2 * n * cap * width * units,
        )[0][None]

    grad_gate = weight_grad([f[1] for f in forward], [b[1] for b in backward])
    grad_up = weight_grad([f[1] for f in forward], [b[2] for b in backward])
    grad_down = weight_grad([b[0] for b in backward], [f[4] for f in forward])
    return (mixed, grad_tokens, grad_gate, grad_up, grad_down)


def per_device(tokens, cotangent, routes, combine, w_gate, w_up, w_down):
    n = lax.axis_size("expert")
    tok, width = tokens.shape
    top = routes.shape[1]
    ring = (
        lax.axis_size("dp") == 1
        and w_gate.shape[0] == 1
        and n % 4 == 0
        and n <= 2 * top
        and tok % 128 == 0
        and top % 8 == 0
        and width >= 3 * tok
        and (tok * top) % (16 * n) == 0
    )
    plan = by_ring if ring else by_all_to_all
    return plan(tokens, cotangent, routes, combine, w_gate, w_up, w_down)


def solution(mesh):
    placed = (
        P(("groups", "expert", "dp"), None),
        P(("groups", "expert", "dp"), None),
        P(("groups", "expert", "dp"), None),
        P(("groups", "expert", "dp"), None),
        P("expert", None, None),
        P("expert", None, None),
        P("expert", None, None),
    )
    return jax.shard_map(
        per_device,
        mesh=mesh,
        in_specs=placed,
        out_specs=(
            P(("groups", "expert", "dp"), None),
            P(("groups", "expert", "dp"), None),
            P(("groups", "expert"), "dp", None),
            P(("groups", "expert"), "dp", None),
            P(("groups", "expert"), "dp", None),
        ),
        check_vma=False,
    )
```

```python
import functools

import jax
import jax.numpy as jnp
from jax import lax
from jax.experimental import pallas as pl
from jax.experimental.pallas import tpu as pltpu
from jax.sharding import PartitionSpec as P

F32 = jnp.float32
BF16 = jnp.bfloat16


def contract_last(left, right):
    return lax.dot_general(
        left, right, (((1,), (1,)), ((), ())), preferred_element_type=jnp.float32
    )


def contract_first(left, right):
    return lax.dot_general(
        left, right, (((0,), (0,)), ((), ())), preferred_element_type=jnp.float32
    )


def by_all_to_all(tokens, cotangent, routes, combine, w_gate, w_up, w_down):
    tok_dev, width = tokens.shape
    top_count = routes.shape[1]
    experts = w_gate.shape[0] * lax.axis_size("expert")
    capacity = min(tok_dev, max(2, (tok_dev * top_count + experts - 1) // experts))
    flat = routes.reshape(-1)
    onehot = (flat[:, None] == jnp.arange(experts, dtype=jnp.int32)[None, :]).astype(jnp.int32)
    rank = jnp.cumsum(onehot, axis=0) - onehot
    place = flat * capacity + jnp.sum(rank * onehot, axis=1)
    owner = jnp.arange(tok_dev * top_count, dtype=jnp.int32) // top_count

    def fill_slots(values):
        empty = jnp.zeros((experts * capacity, width), jnp.bfloat16)
        return empty.at[place].set(values).reshape(experts, capacity, width)

    def collect(returned):
        picked = returned.reshape(-1, width)[place].astype(jnp.float32)
        return picked.reshape(tok_dev, top_count, width)

    outgoing = fill_slots(tokens[owner])
    weighted = (combine.reshape(-1)[:, None] * cotangent[owner].astype(jnp.float32)).astype(
        jnp.bfloat16
    )
    arrived = lax.all_to_all(outgoing, "expert", split_axis=0, concat_axis=0, tiled=True)
    rows = arrived.reshape(-1, width)
    gate_w = w_gate[0]
    up_w = w_up[0]
    down_w = w_down[0]
    gate = jnp.dot(rows, gate_w, preferred_element_type=jnp.float32)
    up = jnp.dot(rows, up_w, preferred_element_type=jnp.float32)
    sig = jax.nn.sigmoid(gate)
    act = gate * sig
    hidden = (act * up).astype(jnp.bfloat16)
    produced = contract_last(hidden, down_w).astype(jnp.bfloat16).reshape(arrived.shape)
    returned = lax.all_to_all(produced, "expert", split_axis=0, concat_axis=0, tiled=True)
    mixed = jnp.sum(collect(returned) * combine[:, :, None], axis=1).astype(jnp.bfloat16)
    grad_arrived = lax.all_to_all(
        fill_slots(weighted), "expert", split_axis=0, concat_axis=0, tiled=True
    )
    grad_rows = grad_arrived.reshape(-1, width)
    dhidden = jnp.dot(grad_rows, down_w, preferred_element_type=jnp.float32)
    dgate = (dhidden * up * sig * (1.0 + gate * (1.0 - sig))).astype(jnp.bfloat16)
    dup = (dhidden * act).astype(jnp.bfloat16)
    dinput = (contract_last(dgate, gate_w) + contract_last(dup, up_w)).astype(jnp.bfloat16)
    back = lax.all_to_all(
        dinput.reshape(arrived.shape), "expert", split_axis=0, concat_axis=0, tiled=True
    )
    grad_tokens = jnp.sum(collect(back), axis=1).astype(jnp.bfloat16)
    summed = lax.psum_scatter(
        jnp.concatenate(
            [
                contract_first(rows, dgate),
                contract_first(rows, dup),
                contract_first(grad_rows, hidden),
            ],
            axis=1,
        ).astype(jnp.bfloat16),
        "dp",
        scatter_dimension=0,
        tiled=True,
    ).astype(jnp.float32)
    hidden_units = gate_w.shape[1]
    grad_gate = summed[:, :hidden_units].astype(jnp.bfloat16)[None]
    grad_up = summed[:, hidden_units : 2 * hidden_units].astype(jnp.bfloat16)[None]
    grad_down = summed[:, 2 * hidden_units :].astype(jnp.bfloat16)[None]
    return (mixed, grad_tokens, grad_gate, grad_up, grad_down)


VMEM = pltpu.VMEM
LIMIT = 20 * 1024 * 1024


def call(body, outs, operands, flops, smem=0, scratch=(), nbytes=None, far=False):
    specs = [pl.BlockSpec(memory_space=pltpu.SMEM)] * smem
    specs += [pl.BlockSpec(memory_space=pltpu.HBM if far else VMEM)] * (len(operands) - smem)
    if far:
        operands = [pltpu.with_memory_space_constraint(a, pltpu.HBM) for a in operands]
    return pl.pallas_call(
        body,
        out_shape=list(outs),
        in_specs=specs,
        out_specs=[pl.BlockSpec(memory_space=VMEM)] * len(outs),
        scratch_shapes=list(scratch),
        compiler_params=pltpu.CompilerParams(vmem_limit_bytes=LIMIT),
        cost_estimate=pl.CostEstimate(flops=0, bytes_accessed=1 << 20, transcendentals=0),
    )(*operands)


def picks(place, cap):
    slots = lax.broadcasted_iota(jnp.int32, (cap, place.shape[1]), 0).astype(F32)
    return jnp.where(slots == place, 1.0, 0.0)


def joined(parts):
    return parts[0] if len(parts) == 1 else jnp.concatenate(parts, axis=0)


def payload_body(routes_hbm, combine_hbm, tokens_hbm, out_ref, routes_ref, combine_ref, sems):
    top, tok = routes_ref.shape
    head = 2 * top
    body = pltpu.make_async_copy(tokens_hbm, out_ref.at[pl.ds(head, tok)], sems.at[0])
    names = pltpu.make_async_copy(routes_hbm, routes_ref, sems.at[1])
    shares = pltpu.make_async_copy(combine_hbm, combine_ref, sems.at[2])
    names.start()
    shares.start()
    body.start()
    out_ref[:head] = jnp.zeros((head, out_ref.shape[1]), BF16)
    names.wait()
    shares.wait()
    exact = combine_ref[...]
    high = exact.astype(BF16)
    rest = exact - high.astype(F32)
    middle = rest.astype(BF16)
    low = (rest - middle.astype(F32)).astype(BF16)
    blank = jnp.zeros((top, tok), F32)
    named = jnp.concatenate([routes_ref[...].astype(F32), high.astype(F32)], axis=0)
    out_ref[:head, :tok] = named.astype(BF16)
    for i, term in enumerate((middle, low)):
        padded = jnp.concatenate([blank, term.astype(F32)], axis=0)
        out_ref[:head, (i + 1) * tok : (i + 2) * tok] = padded.astype(BF16)
    body.wait()


def stage_body(*refs):
    *pairs, sems = refs
    half = len(pairs) // 2
    copies = [
        pltpu.make_async_copy(pairs[i], pairs[half + i], sems.at[i]) for i in range(half)
    ]
    for copy in copies:
        copy.start()
    for copy in copies:
        copy.wait()


def forward_body(cap, top, kept, expert_ref, near, far, w_gate, w_up, w_down, *outs):
    info_ref, rows_ref, slope_ref, act_ref, hidden_ref, keep_ref, give_ref = outs
    me = expert_ref[0].astype(F32)
    mate = expert_ref[1].astype(F32)
    head = 2 * top
    tok = info_ref.shape[1]
    tall = head + tok
    blocks = [(side, low) for side in (near, far) for low in range(0, side.shape[0], tall)]
    names, terms = [], []
    for side, low in blocks:
        told = side[low : low + head, : 3 * tok].astype(F32)
        names.append(told[:top, :tok])
        told = told[top:]
        terms.append(told[:, :tok] + (told[:, tok : 2 * tok] + told[:, 2 * tok :]))
    masks, weights = [], []
    for expert, which in [(me, i) for i in range(len(blocks))] + [(mate, i) for i in kept]:
        hit = names[which] == expert
        masks.append(jnp.sum(jnp.where(hit, 1.0, 0.0), axis=0, keepdims=True))
        weights.append(jnp.sum(jnp.where(hit, terms[which], 0.0), axis=0, keepdims=True))
    pad = jnp.zeros((8 - len(masks), tok), F32)
    mask = jnp.concatenate(masks + [pad], axis=0)
    before = lax.broadcasted_iota(jnp.int32, (tok, tok), 0) < lax.broadcasted_iota(
        jnp.int32, (tok, tok), 1
    )
    rank = jnp.dot(
        mask.astype(BF16), jnp.where(before, 1.0, 0.0).astype(BF16), preferred_element_type=F32
    )
    place = jnp.where(mask > 0.5, rank, -1.0)
    info_ref[0:8] = place
    info_ref[8:16] = jnp.concatenate(weights + [pad], axis=0)
    share = []
    for i, (side, low) in enumerate(blocks):
        pick = picks(place[i : i + 1], cap)
        share.append(jnp.sum(pick * weights[i], axis=1, keepdims=True))
        taken = jnp.dot(
            pick.astype(BF16), side[low + head : low + tall], preferred_element_type=F32
        )
        rows_ref[i * cap : (i + 1) * cap] = taken.astype(BF16)
    rows = rows_ref[...]
    gate = jnp.dot(rows, w_gate[...], preferred_element_type=F32)
    up = jnp.dot(rows, w_up[...], preferred_element_type=F32)
    sig = jax.nn.sigmoid(gate)
    act = gate * sig
    hidden = (act * up).astype(BF16)
    hidden_ref[...] = hidden
    act_ref[...] = act
    slope_ref[...] = up * sig * (1.0 + gate * (1.0 - sig))
    produced = contract_last(hidden, w_down[...]).astype(BF16).astype(F32)
    split(kept, cap, (jnp.concatenate(share, axis=0) * produced).astype(BF16), keep_ref, give_ref)


def split(kept, cap, rows, keep_ref, give_ref):
    cut = rows.shape[0] // 2
    first, second = (keep_ref, give_ref) if kept[0] == 0 else (give_ref, keep_ref)
    first[...] = rows[:cut]
    second[...] = rows[cut:]


def backward_body(cap, kept, info_ref, slope, act, near, far, w_gate, w_up, w_down, *outs):
    rows_ref, dgate_ref, dup_ref, keep_ref, give_ref = outs
    tok = info_ref.shape[1]
    blocks = [(side, low) for side in (near, far) for low in range(0, side.shape[0], tok)]
    for i, (side, low) in enumerate(blocks):
        pick = picks(info_ref[i : i + 1], cap)
        share = jnp.sum(pick * info_ref[8 + i : 9 + i], axis=1, keepdims=True)
        taken = jnp.dot(pick.astype(BF16), side[low : low + tok], preferred_element_type=F32)
        rows_ref[i * cap : (i + 1) * cap] = (share * taken).astype(BF16)
    dhidden = jnp.dot(rows_ref[...], w_down[...], preferred_element_type=F32)
    dgate = (dhidden * slope[...]).astype(BF16)
    dup = (dhidden * act[...]).astype(BF16)
    dgate_ref[...] = dgate
    dup_ref[...] = dup
    back = contract_last(dgate, w_gate[...]) + contract_last(dup, w_up[...])
    split(kept, cap, back.astype(BF16), keep_ref, give_ref)


def return_body(cap, kept, count, info_ref, keep, give, *refs):
    arrived, outs = refs[: len(refs) - count], refs[len(refs) - count :]
    tok = info_ref.shape[1]
    sums = []
    for j in reversed(range(len(kept))):
        i = kept[j]
        mate = 2 * len(kept) + j
        both = jnp.concatenate(
            [picks(info_ref[i : i + 1], cap), picks(info_ref[mate : mate + 1], cap)], axis=0
        ).astype(BF16)
        part = slice(j * cap, (j + 1) * cap)
        sums.append(contract_first(both, jnp.concatenate([keep[part], give[part]], axis=0)))
    for ref in arrived:
        for j in range(ref.shape[0] // tok):
            sums[j] = sums[j] + ref[j * tok : (j + 1) * tok].astype(F32)
    for out, total in zip(outs, sums if count > 1 else [joined(sums)]):
        out[...] = total.astype(BF16)


def weights_body(steps, cols, *refs):
    rows = refs[:steps]
    grads = refs[steps : 2 * steps]
    out = refs[2 * steps]
    right = jnp.concatenate([g[...] for g in grads], axis=0)
    for low in range(0, out.shape[0], cols):
        left = jnp.concatenate([r[:, low : low + cols] for r in rows], axis=0)
        out[low : low + cols] = contract_first(left, right).astype(BF16)


def by_ring(tokens, cotangent, routes, combine, w_gate, w_up, w_down):
    tok, width = tokens.shape
    top = routes.shape[1]
    n = lax.axis_size("expert")
    cap = (tok * top + n - 1) // n
    units = w_gate.shape[2]
    gate_w, up_w, down_w = w_gate[0], w_up[0], w_down[0]
    pairs = n // 2
    reach = pairs // 2
    walk = [2 * i for i in range(reach)] + [2 * i + 1 for i in reversed(range(reach))]
    straight = [
        (2 * walk[i] + core, 2 * walk[(i + 1 - 2 * core) % pairs] + core)
        for i in range(pairs)
        for core in range(2)
    ]
    crossing = [
        (2 * walk[i] + core, 2 * walk[(i - 1 + 2 * core) % pairs] + 1 - core)
        for i in range(pairs)
        for core in range(2)
    ]
    crossing_back = [(a, b ^ 1) for a, b in straight]

    def hop(value, what, moves=straight):
        with jax.named_scope(what):
            return lax.ppermute(value, "expert", moves)

    def swap(value, what):
        return hop(value, what, [(i, i ^ 1) for i in range(n)])

    def after(value, *others):
        return lax.optimization_barrier((value, *others))[0] if others else value

    def land(values, *before):
        return list(lax.optimization_barrier((*values, *before))[: len(values)])

    def struct(shape, dtype):
        return jax.ShapeDtypeStruct(shape, dtype)

    here = lax.axis_index("expert").astype(jnp.int32)
    expert = jnp.stack([here, here ^ 1])
    head = 2 * top

    def blocks_of(step):
        return (4, (2, 3)) if 0 < step < reach else (2, (0,))

    def run_forward(step):
        count, kept = blocks_of(step)
        m = count * cap
        return call(
            functools.partial(forward_body, cap, top, kept),
            [
                struct((16, tok), F32),
                struct((m, width), BF16),
                struct((m, units), F32),
                struct((m, units), F32),
                struct((m, units), BF16),
                struct((m // 2, width), BF16),
                struct((m // 2, width), BF16),
            ],
            [expert, token_near[step], token_far[step], gate_w, up_w, down_w],
            0,
            smem=1,
        )

    def run_backward(step):
        count, kept = blocks_of(step)
        m = count * cap
        info, _, slope, act = forward[step][:4]
        return call(
            functools.partial(backward_body, cap, kept),
            [
                struct((m, width), BF16),
                struct((m, units), BF16),
                struct((m, units), BF16),
                struct((m // 2, width), BF16),
                struct((m // 2, width), BF16),
            ],
            [info, slope, act, cot_near[step], cot_far[step], gate_w, up_w, down_w],
            0,
        )

    payload = call(
        payload_body,
        [struct((head + tok, width), BF16)],
        [routes.T, combine.T, tokens],
        0,
        scratch=[VMEM((top, tok), jnp.int32), VMEM((top, tok), F32), pltpu.SemaphoreType.DMA((3,))],
        far=True,
    )[0]
    staged = after((gate_w, up_w, down_w), payload)
    gate_w, up_w, down_w = call(
        stage_body,
        [struct(w.shape, BF16) for w in staged],
        staged,
        0,
        scratch=[pltpu.SemaphoreType.DMA((3,))],
        far=True,
    )

    def depart(block, what):
        return [hop(block, what + "_1"), hop(block, what + "_1_crossing", crossing)]

    def onward(near, step, what):
        if step == reach:
            near = near[: near.shape[0] // 2]
        return [hop(near, f"{what}_{step}")]

    cot = after(cotangent, payload)
    token_near, cot_near = [payload], [cot]
    token_fly, cot_fly = depart(payload, "tokens"), depart(cot, "cotangent")
    token_far, cot_far = [swap(payload, "tokens_0_swap")], [swap(cot, "cotangent_0_swap")]
    forward, backward = [], []
    for step in range(1, reach + 1):
        before = [b[1] for b in backward[-1:]] or [gate_w]
        *arrived, token_near[-1] = land([*token_fly, token_near[-1]], *before)
        token_near.append(joined(arrived))
        if step < reach:
            token_fly = onward(token_near[-1], step + 1, "tokens")
        token_far.append(swap(token_near[-1], f"tokens_{step}_swap"))
        forward.append(run_forward(step - 1))
        if step == reach:
            forward.append(run_forward(reach))
        before = [f[5] for f in forward[step - 1 :]]
        *arrived, cot_near[-1] = land([*cot_fly, cot_near[-1]], *before)
        cot_near.append(joined(arrived))
        if step < reach:
            cot_fly = onward(cot_near[-1], step + 1, "cotangent")
        cot_far.append(swap(cot_near[-1], f"cotangent_{step}_swap"))
        backward.append(run_backward(step - 1))
    backward.append(run_backward(reach))

    def back_from(step, kept, given, values):
        outs = {0: (tok,), 1: (tok, tok), reach: (tok,)}.get(step, (2 * tok,))
        return call(
            functools.partial(return_body, cap, blocks_of(step)[1], len(outs)),
            [struct((rows, width), BF16) for rows in outs],
            [forward[step][0], kept[step], given[step], *values],
            0,
        )

    def send_back(sums, step, what):
        if step == 1:
            return [hop(sums[0], what + "_1"), hop(sums[1], what + "_1_crossing", crossing_back)]
        return [hop(sums[0], f"{what}_{step}")]

    def weight_grad(lefts, rights):
        return call(
            functools.partial(weights_body, len(lefts), 256),
            [struct((width, units), BF16)],
            [*lefts, *rights],
            0,
        )[0]

    mixed_kept = [f[5] for f in forward]
    mixed_given = [swap(f[6], f"mixed_{i}_swap") for i, f in enumerate(forward)]
    grad_kept = [b[3] for b in backward]
    grad_given = [swap(b[4], f"grad_{i}_swap") for i, b in enumerate(backward)]

    token_rows = [f[1] for f in forward]
    jobs = [
        (token_rows, [b[1] for b in backward]),
        (token_rows, [b[2] for b in backward]),
        ([b[0] for b in backward], [f[4] for f in forward]),
    ]
    grads = []

    def some_job():
        if len(grads) < len(jobs):
            grads.append(weight_grad(*jobs[len(grads)]))
            return grads[-1:]
        return []

    left = back_from(reach, mixed_kept, mixed_given, ())
    mixed_fly = send_back(left, reach, "mixed")
    left = back_from(reach, grad_kept, grad_given, ())
    grad_fly = send_back(left, reach, "grad")
    for step in range(reach - 1, 0, -1):
        arrived = land(mixed_fly, *left, *(some_job() if step < reach - 1 else []))
        left = back_from(step, mixed_kept, mixed_given, arrived)
        mixed_fly = send_back(left, step, "mixed")
        arrived = land(grad_fly, *left, *(some_job() if step < reach - 1 else []))
        left = back_from(step, grad_kept, grad_given, arrived)
        grad_fly = send_back(left, step, "grad")
    while len(grads) < len(jobs):
        some_job()
    mixed = back_from(0, mixed_kept, mixed_given, land(mixed_fly, *left, *grads))[0]
    grad_tokens = back_from(0, grad_kept, grad_given, land(grad_fly, mixed))[0]
    return (mixed, grad_tokens, *[g[None] for g in grads])


def per_device(tokens, cotangent, routes, combine, w_gate, w_up, w_down):
    n = lax.axis_size("expert")
    tok, width = tokens.shape
    top = routes.shape[1]
    ring = (
        lax.axis_size("dp") == 1
        and w_gate.shape[0] == 1
        and n % 4 == 0
        and n >= 8
        and n <= 2 * top
        and tok % 128 == 0
        and top % 8 == 0
        and width >= 3 * tok
        and (tok * top) % (16 * n) == 0
    )
    plan = by_ring if ring else by_all_to_all
    return plan(tokens, cotangent, routes, combine, w_gate, w_up, w_down)


def solution(mesh):
    placed = (
        P(("groups", "expert", "dp"), None),
        P(("groups", "expert", "dp"), None),
        P(("groups", "expert", "dp"), None),
        P(("groups", "expert", "dp"), None),
        P("expert", None, None),
        P("expert", None, None),
        P("expert", None, None),
    )
    return jax.shard_map(
        per_device,
        mesh=mesh,
        in_specs=placed,
        out_specs=(
            P(("groups", "expert", "dp"), None),
            P(("groups", "expert", "dp"), None),
            P(("groups", "expert"), "dp", None),
            P(("groups", "expert"), "dp", None),
            P(("groups", "expert"), "dp", None),
        ),
        check_vma=False,
    )
```

```python
import functools

import jax
import jax.numpy as jnp
from jax import lax
from jax.experimental import pallas as pl
from jax.experimental.pallas import tpu as pltpu
from jax.sharding import PartitionSpec as P

F32 = jnp.float32
BF16 = jnp.bfloat16


def contract_last(left, right):
    return lax.dot_general(
        left, right, (((1,), (1,)), ((), ())), preferred_element_type=jnp.float32
    )


def contract_first(left, right):
    return lax.dot_general(
        left, right, (((0,), (0,)), ((), ())), preferred_element_type=jnp.float32
    )


def by_all_to_all(tokens, cotangent, routes, combine, w_gate, w_up, w_down):
    tok_dev, width = tokens.shape
    top_count = routes.shape[1]
    experts = w_gate.shape[0] * lax.axis_size("expert")
    capacity = min(tok_dev, max(2, (tok_dev * top_count + experts - 1) // experts))
    flat = routes.reshape(-1)
    onehot = (flat[:, None] == jnp.arange(experts, dtype=jnp.int32)[None, :]).astype(jnp.int32)
    rank = jnp.cumsum(onehot, axis=0) - onehot
    place = flat * capacity + jnp.sum(rank * onehot, axis=1)
    owner = jnp.arange(tok_dev * top_count, dtype=jnp.int32) // top_count

    def fill_slots(values):
        empty = jnp.zeros((experts * capacity, width), jnp.bfloat16)
        return empty.at[place].set(values).reshape(experts, capacity, width)

    def collect(returned):
        picked = returned.reshape(-1, width)[place].astype(jnp.float32)
        return picked.reshape(tok_dev, top_count, width)

    outgoing = fill_slots(tokens[owner])
    weighted = (combine.reshape(-1)[:, None] * cotangent[owner].astype(jnp.float32)).astype(
        jnp.bfloat16
    )
    arrived = lax.all_to_all(outgoing, "expert", split_axis=0, concat_axis=0, tiled=True)
    rows = arrived.reshape(-1, width)
    gate_w = w_gate[0]
    up_w = w_up[0]
    down_w = w_down[0]
    gate = jnp.dot(rows, gate_w, preferred_element_type=jnp.float32)
    up = jnp.dot(rows, up_w, preferred_element_type=jnp.float32)
    sig = jax.nn.sigmoid(gate)
    act = gate * sig
    hidden = (act * up).astype(jnp.bfloat16)
    produced = contract_last(hidden, down_w).astype(jnp.bfloat16).reshape(arrived.shape)
    returned = lax.all_to_all(produced, "expert", split_axis=0, concat_axis=0, tiled=True)
    mixed = jnp.sum(collect(returned) * combine[:, :, None], axis=1).astype(jnp.bfloat16)
    grad_arrived = lax.all_to_all(
        fill_slots(weighted), "expert", split_axis=0, concat_axis=0, tiled=True
    )
    grad_rows = grad_arrived.reshape(-1, width)
    dhidden = jnp.dot(grad_rows, down_w, preferred_element_type=jnp.float32)
    dgate = (dhidden * up * sig * (1.0 + gate * (1.0 - sig))).astype(jnp.bfloat16)
    dup = (dhidden * act).astype(jnp.bfloat16)
    dinput = (contract_last(dgate, gate_w) + contract_last(dup, up_w)).astype(jnp.bfloat16)
    back = lax.all_to_all(
        dinput.reshape(arrived.shape), "expert", split_axis=0, concat_axis=0, tiled=True
    )
    grad_tokens = jnp.sum(collect(back), axis=1).astype(jnp.bfloat16)
    summed = lax.psum_scatter(
        jnp.concatenate(
            [
                contract_first(rows, dgate),
                contract_first(rows, dup),
                contract_first(grad_rows, hidden),
            ],
            axis=1,
        ).astype(jnp.bfloat16),
        "dp",
        scatter_dimension=0,
        tiled=True,
    ).astype(jnp.float32)
    hidden_units = gate_w.shape[1]
    grad_gate = summed[:, :hidden_units].astype(jnp.bfloat16)[None]
    grad_up = summed[:, hidden_units : 2 * hidden_units].astype(jnp.bfloat16)[None]
    grad_down = summed[:, 2 * hidden_units :].astype(jnp.bfloat16)[None]
    return (mixed, grad_tokens, grad_gate, grad_up, grad_down)


VMEM = pltpu.VMEM
LIMIT = 20 * 1024 * 1024


def call(body, outs, operands, flops, smem=0, scratch=(), near=True, far=False):
    specs = [pl.BlockSpec(memory_space=pltpu.SMEM)] * smem
    specs += [pl.BlockSpec(memory_space=pltpu.HBM if far else VMEM)] * (len(operands) - smem)
    if far:
        operands = [pltpu.with_memory_space_constraint(a, pltpu.HBM) for a in operands]
    return pl.pallas_call(
        body,
        out_shape=[pltpu.VMEM(a.shape, a.dtype) if near else a for a in outs],
        in_specs=specs,
        out_specs=[pl.BlockSpec(memory_space=VMEM)] * len(outs),
        scratch_shapes=list(scratch),
        compiler_params=pltpu.CompilerParams(vmem_limit_bytes=LIMIT),
        cost_estimate=pl.CostEstimate(flops=1 << 20, bytes_accessed=1 << 10, transcendentals=0),
    )(*operands)


def picks(place, cap):
    slots = lax.broadcasted_iota(jnp.int32, (cap, place.shape[1]), 0).astype(F32)
    return jnp.where(slots == place, 1.0, 0.0)


def joined(parts):
    return parts[0] if len(parts) == 1 else jnp.concatenate(parts, axis=0)


def payload_body(routes_hbm, combine_hbm, tokens_hbm, out_ref, routes_ref, combine_ref, sems):
    top, tok = routes_ref.shape
    head = 2 * top
    body = pltpu.make_async_copy(tokens_hbm, out_ref.at[pl.ds(head, tok)], sems.at[0])
    names = pltpu.make_async_copy(routes_hbm, routes_ref, sems.at[1])
    shares = pltpu.make_async_copy(combine_hbm, combine_ref, sems.at[2])
    names.start()
    shares.start()
    body.start()
    out_ref[:head] = jnp.zeros((head, out_ref.shape[1]), BF16)
    names.wait()
    shares.wait()
    exact = combine_ref[...]
    high = exact.astype(BF16)
    rest = exact - high.astype(F32)
    middle = rest.astype(BF16)
    low = (rest - middle.astype(F32)).astype(BF16)
    blank = jnp.zeros((top, tok), F32)
    named = jnp.concatenate([routes_ref[...].astype(F32), high.astype(F32)], axis=0)
    out_ref[:head, :tok] = named.astype(BF16)
    for i, term in enumerate((middle, low)):
        padded = jnp.concatenate([blank, term.astype(F32)], axis=0)
        out_ref[:head, (i + 1) * tok : (i + 2) * tok] = padded.astype(BF16)
    body.wait()


def join_body(head, tok, first, second, out):
    if head:
        reach = 3 * tok
        out[:head] = first[:head]
        out[:head, 4 * tok : 4 * tok + reach] = second[:head, :reach]
    out[head : head + tok] = first[head:]
    out[head + tok :] = second[head:]


def stage_body(*refs):
    *pairs, sems = refs
    half = len(pairs) // 2
    copies = [
        pltpu.make_async_copy(pairs[i], pairs[half + i], sems.at[i]) for i in range(half)
    ]
    for copy in copies:
        copy.start()
    for copy in copies:
        copy.wait()


def forward_body(cap, top, kept, expert_ref, near, far, w_gate, w_up, w_down, *outs):
    info_ref, rows_ref, slope_ref, act_ref, hidden_ref, keep_ref, give_ref = outs
    me = expert_ref[0].astype(F32)
    mate = expert_ref[1].astype(F32)
    head = 2 * top
    tok = info_ref.shape[1]
    blocks = [(side, j) for side in (near, far) for j in range((side.shape[0] - head) // tok)]
    names, terms = [], []
    for side, j in blocks:
        told = side[:head, 4 * tok * j : 4 * tok * j + 3 * tok].astype(F32)
        names.append(told[:top, :tok])
        told = told[top:]
        terms.append(told[:, :tok] + (told[:, tok : 2 * tok] + told[:, 2 * tok :]))
    masks, weights = [], []
    for expert, which in [(me, i) for i in range(len(blocks))] + [(mate, i) for i in kept]:
        hit = names[which] == expert
        masks.append(jnp.sum(jnp.where(hit, 1.0, 0.0), axis=0, keepdims=True))
        weights.append(jnp.sum(jnp.where(hit, terms[which], 0.0), axis=0, keepdims=True))
    pad = jnp.zeros((8 - len(masks), tok), F32)
    mask = jnp.concatenate(masks + [pad], axis=0)
    before = lax.broadcasted_iota(jnp.int32, (tok, tok), 0) < lax.broadcasted_iota(
        jnp.int32, (tok, tok), 1
    )
    rank = jnp.dot(
        mask.astype(BF16), jnp.where(before, 1.0, 0.0).astype(BF16), preferred_element_type=F32
    )
    place = jnp.where(mask > 0.5, rank, -1.0)
    info_ref[0:8] = place
    info_ref[8:16] = jnp.concatenate(weights + [pad], axis=0)
    share = []
    for i, (side, j) in enumerate(blocks):
        low = head + j * tok
        pick = picks(place[i : i + 1], cap)
        share.append(jnp.sum(pick * weights[i], axis=1, keepdims=True))
        taken = jnp.dot(
            pick.astype(BF16), side[low : low + tok], preferred_element_type=F32
        )
        rows_ref[i * cap : (i + 1) * cap] = taken.astype(BF16)
    rows = rows_ref[...]
    gate = jnp.dot(rows, w_gate[...], preferred_element_type=F32)
    up = jnp.dot(rows, w_up[...], preferred_element_type=F32)
    sig = jax.nn.sigmoid(gate)
    act = gate * sig
    hidden = (act * up).astype(BF16)
    hidden_ref[...] = hidden
    act_ref[...] = act
    slope_ref[...] = up * sig * (1.0 + gate * (1.0 - sig))
    produced = contract_last(hidden, w_down[...]).astype(BF16).astype(F32)
    split(kept, cap, (jnp.concatenate(share, axis=0) * produced).astype(BF16), keep_ref, give_ref)


def split(kept, cap, rows, keep_ref, give_ref):
    cut = rows.shape[0] // 2
    first, second = (keep_ref, give_ref) if kept[0] == 0 else (give_ref, keep_ref)
    first[...] = rows[:cut]
    second[...] = rows[cut:]


def backward_body(cap, kept, info_ref, slope, act, near, far, w_gate, w_up, w_down, *outs):
    rows_ref, dgate_ref, dup_ref, keep_ref, give_ref = outs
    tok = info_ref.shape[1]
    blocks = [(side, low) for side in (near, far) for low in range(0, side.shape[0], tok)]
    for i, (side, low) in enumerate(blocks):
        pick = picks(info_ref[i : i + 1], cap)
        share = jnp.sum(pick * info_ref[8 + i : 9 + i], axis=1, keepdims=True)
        taken = jnp.dot(pick.astype(BF16), side[low : low + tok], preferred_element_type=F32)
        rows_ref[i * cap : (i + 1) * cap] = (share * taken).astype(BF16)
    dhidden = jnp.dot(rows_ref[...], w_down[...], preferred_element_type=F32)
    dgate = (dhidden * slope[...]).astype(BF16)
    dup = (dhidden * act[...]).astype(BF16)
    dgate_ref[...] = dgate
    dup_ref[...] = dup
    back = contract_last(dgate, w_gate[...]) + contract_last(dup, w_up[...])
    split(kept, cap, back.astype(BF16), keep_ref, give_ref)


def return_body(cap, kept, count, info_ref, keep, give, *refs):
    arrived, outs = refs[: len(refs) - count], refs[len(refs) - count :]
    tok = info_ref.shape[1]
    sums = []
    for j in reversed(range(len(kept))):
        i = kept[j]
        mate = 2 * len(kept) + j
        both = jnp.concatenate(
            [picks(info_ref[i : i + 1], cap), picks(info_ref[mate : mate + 1], cap)], axis=0
        ).astype(BF16)
        part = slice(j * cap, (j + 1) * cap)
        sums.append(contract_first(both, jnp.concatenate([keep[part], give[part]], axis=0)))
    for ref in arrived:
        for j in range(ref.shape[0] // tok):
            sums[j] = sums[j] + ref[j * tok : (j + 1) * tok].astype(F32)
    for out, total in zip(outs, sums if count > 1 else [joined(sums)]):
        out[...] = total.astype(BF16)


def weights_body(steps, cols, *refs):
    rows = refs[:steps]
    grads = refs[steps : 2 * steps]
    out = refs[2 * steps]
    right = jnp.concatenate([g[...] for g in grads], axis=0)
    for low in range(0, out.shape[0], cols):
        left = jnp.concatenate([r[:, low : low + cols] for r in rows], axis=0)
        out[low : low + cols] = contract_first(left, right).astype(BF16)


def by_ring(tokens, cotangent, routes, combine, w_gate, w_up, w_down):
    tok, width = tokens.shape
    top = routes.shape[1]
    n = lax.axis_size("expert")
    cap = (tok * top + n - 1) // n
    units = w_gate.shape[2]
    gate_w, up_w, down_w = w_gate[0], w_up[0], w_down[0]
    pairs = n // 2
    reach = pairs // 2
    walk = [2 * i for i in range(reach)] + [2 * i + 1 for i in reversed(range(reach))]
    straight = [
        (2 * walk[i] + core, 2 * walk[(i + 1 - 2 * core) % pairs] + core)
        for i in range(pairs)
        for core in range(2)
    ]
    crossing = [
        (2 * walk[i] + core, 2 * walk[(i - 1 + 2 * core) % pairs] + 1 - core)
        for i in range(pairs)
        for core in range(2)
    ]
    crossing_back = [(a, b ^ 1) for a, b in straight]

    def hop(value, what, moves=straight):
        with jax.named_scope(what):
            return lax.ppermute(value, "expert", moves)

    def swap(value, what):
        return hop(value, what, [(i, i ^ 1) for i in range(n)])

    def after(value, *others):
        return lax.optimization_barrier((value, *others))[0] if others else value

    def land(values, *before):
        return list(lax.optimization_barrier((*values, *before))[: len(values)])

    def struct(shape, dtype):
        return jax.ShapeDtypeStruct(shape, dtype)

    here = lax.axis_index("expert").astype(jnp.int32)
    expert = jnp.stack([here, here ^ 1])
    head = 2 * top

    def blocks_of(step):
        return (4, (2, 3)) if 0 < step < reach else (2, (0,))

    def run_forward(step):
        count, kept = blocks_of(step)
        m = count * cap
        return call(
            functools.partial(forward_body, cap, top, kept),
            [
                struct((16, tok), F32),
                struct((m, width), BF16),
                struct((m, units), F32),
                struct((m, units), F32),
                struct((m, units), BF16),
                struct((m // 2, width), BF16),
                struct((m // 2, width), BF16),
            ],
            [expert, token_near[step], token_far[step], gate_w, up_w, down_w],
            0,
            smem=1,
        )

    def run_backward(step):
        count, kept = blocks_of(step)
        m = count * cap
        info, _, slope, act = forward[step][:4]
        return call(
            functools.partial(backward_body, cap, kept),
            [
                struct((m, width), BF16),
                struct((m, units), BF16),
                struct((m, units), BF16),
                struct((m // 2, width), BF16),
                struct((m // 2, width), BF16),
            ],
            [info, slope, act, cot_near[step], cot_far[step], gate_w, up_w, down_w],
            0,
        )

    payload = call(
        payload_body,
        [struct((head + tok, width), BF16)],
        [routes.T, combine.T, tokens],
        0,
        scratch=[VMEM((top, tok), jnp.int32), VMEM((top, tok), F32), pltpu.SemaphoreType.DMA((3,))],
        far=True,
    )[0]
    staged = after((gate_w, up_w, down_w), payload)
    gate_w, up_w, down_w = call(
        stage_body,
        [struct(w.shape, BF16) for w in staged],
        staged,
        0,
        scratch=[pltpu.SemaphoreType.DMA((3,))],
        far=True,
    )

    def join(arrived, top_rows):
        if len(arrived) == 1:
            return arrived[0]
        return call(
            functools.partial(join_body, top_rows, tok),
            [struct((top_rows + 2 * tok, width), BF16)],
            arrived,
            0,
        )[0]

    def onward(near, step, top_rows, what):
        if step == reach:
            near = near[: top_rows + tok]
        return [hop(near, f"{what}_{step}")]

    token_near, cot_near = [payload], [cotangent]
    token_fly = [hop(payload, "tokens_1"), hop(payload, "tokens_1_crossing", crossing)]
    token_far, cot_far = [swap(payload, "tokens_0_swap")], [swap(cotangent, "cotangent_0_swap")]
    cot_fly = [hop(join([cotangent, cot_far[0]], 0), "cotangent_1")]
    forward, backward = [], []
    for step in range(1, reach + 1):
        before = [b[1] for b in backward[-1:]] or [gate_w]
        *arrived, token_near[-1] = land([*token_fly, token_near[-1]], *before)
        token_near.append(join(arrived, head))
        if step < reach:
            token_fly = onward(token_near[-1], step + 1, head, "tokens")
        token_far.append(swap(token_near[-1], f"tokens_{step}_swap"))
        forward.append(run_forward(step - 1))
        *arrived, cot_near[-1] = land([*cot_fly, cot_near[-1]], forward[-1][5])
        cot_near.append(join(arrived, 0))
        if step < reach:
            cot_fly = onward(cot_near[-1], step + 1, 0, "cotangent")
        cot_far.append(swap(cot_near[-1], f"cotangent_{step}_swap"))
        if step < reach:
            backward.append(run_backward(step - 1))
    token_near[reach] = after(token_near[reach], cot_near[reach])
    forward.append(run_forward(reach))
    backward.append(run_backward(reach - 1))

    def back_from(step, kept, given, values):
        outs = {0: (tok,), 1: (tok, tok), reach: (tok,)}.get(step, (2 * tok,))
        return call(
            functools.partial(return_body, cap, blocks_of(step)[1], len(outs)),
            [struct((rows, width), BF16) for rows in outs],
            [forward[step][0], kept, given, *values],
            0,
            near=step > 0,
        )

    def send_back(sums, step, what):
        if step == 1:
            return [hop(sums[0], what + "_1"), hop(sums[1], what + "_1_crossing", crossing_back)]
        return [hop(sums[0], f"{what}_{step}")]

    def mixed_swap(step):
        return swap(forward[step][6], f"mixed_{step}_swap")

    def grad_swap(step):
        return swap(backward[step][4], f"grad_{step}_swap")


    def weight_grad(lefts, rights):
        return call(
            functools.partial(weights_body, len(lefts), 256),
            [struct((width, units), BF16)],
            [*lefts, *rights],
            0,
            near=False,
        )[0]

    mixed_kept = after(forward[reach][5], backward[reach - 1][1])
    mixed_left = back_from(reach, mixed_kept, mixed_swap(reach), ())
    mixed_fly = send_back(mixed_left, reach, "mixed")
    cot_near[reach] = after(cot_near[reach], *mixed_left)
    backward.append(run_backward(reach))
    grad_left = back_from(reach, backward[reach][3], grad_swap(reach), ())
    grad_fly = send_back(grad_left, reach, "grad")

    token_rows = [f[1] for f in forward]
    jobs = [
        (token_rows, [b[1] for b in backward]),
        (token_rows, [b[2] for b in backward]),
        ([b[0] for b in backward], [f[4] for f in forward]),
    ]
    grads = []

    def some_job():
        if len(grads) < len(jobs):
            grads.append(weight_grad(*jobs[len(grads)]))
            return grads[-1:]
        return []

    for step in range(reach - 1, 0, -1):
        arrived = land(mixed_fly, *grad_left, *(some_job() if step < reach - 1 else []))
        mixed_left = back_from(step, forward[step][5], mixed_swap(step), arrived)
        mixed_fly = send_back(mixed_left, step, "mixed")
        arrived = land(grad_fly, *mixed_left, *(some_job() if step < reach - 1 else []))
        grad_left = back_from(step, backward[step][3], grad_swap(step), arrived)
        grad_fly = send_back(grad_left, step, "grad")
    while len(grads) < len(jobs):
        some_job()
    arrived = land(mixed_fly, *grad_left, *grads)
    mixed = back_from(0, forward[0][5], mixed_swap(0), arrived)[0]
    arrived = land(grad_fly, mixed)
    grad_tokens = back_from(0, backward[0][3], grad_swap(0), arrived)[0]
    return (mixed, grad_tokens, *[g[None] for g in grads])


def per_device(tokens, cotangent, routes, combine, w_gate, w_up, w_down):
    n = lax.axis_size("expert")
    tok, width = tokens.shape
    top = routes.shape[1]
    ring = (
        lax.axis_size("dp") == 1
        and w_gate.shape[0] == 1
        and n % 4 == 0
        and n >= 8
        and n <= 2 * top
        and tok % 128 == 0
        and top % 8 == 0
        and width >= 8 * tok
        and (tok * top) % (16 * n) == 0
    )
    plan = by_ring if ring else by_all_to_all
    return plan(tokens, cotangent, routes, combine, w_gate, w_up, w_down)


def solution(mesh):
    placed = (
        P(("groups", "expert", "dp"), None),
        P(("groups", "expert", "dp"), None),
        P(("groups", "expert", "dp"), None),
        P(("groups", "expert", "dp"), None),
        P("expert", None, None),
        P("expert", None, None),
        P("expert", None, None),
    )
    return jax.shard_map(
        per_device,
        mesh=mesh,
        in_specs=placed,
        out_specs=(
            P(("groups", "expert", "dp"), None),
            P(("groups", "expert", "dp"), None),
            P(("groups", "expert"), "dp", None),
            P(("groups", "expert"), "dp", None),
            P(("groups", "expert"), "dp", None),
        ),
        check_vma=False,
    )
```

```python
import functools

import jax
import jax.numpy as jnp
from jax import lax
from jax.experimental import pallas as pl
from jax.experimental.pallas import tpu as pltpu
from jax.sharding import PartitionSpec as P

F32 = jnp.float32
BF16 = jnp.bfloat16


def contract_last(left, right):
    return lax.dot_general(
        left, right, (((1,), (1,)), ((), ())), preferred_element_type=jnp.float32
    )


def contract_first(left, right):
    return lax.dot_general(
        left, right, (((0,), (0,)), ((), ())), preferred_element_type=jnp.float32
    )


def by_all_to_all(tokens, cotangent, routes, combine, w_gate, w_up, w_down):
    tok_dev, width = tokens.shape
    top_count = routes.shape[1]
    experts = w_gate.shape[0] * lax.axis_size("expert")
    capacity = min(tok_dev, max(2, (tok_dev * top_count + experts - 1) // experts))
    flat = routes.reshape(-1)
    onehot = (flat[:, None] == jnp.arange(experts, dtype=jnp.int32)[None, :]).astype(jnp.int32)
    rank = jnp.cumsum(onehot, axis=0) - onehot
    place = flat * capacity + jnp.sum(rank * onehot, axis=1)
    owner = jnp.arange(tok_dev * top_count, dtype=jnp.int32) // top_count

    def fill_slots(values):
        empty = jnp.zeros((experts * capacity, width), jnp.bfloat16)
        return empty.at[place].set(values).reshape(experts, capacity, width)

    def collect(returned):
        picked = returned.reshape(-1, width)[place].astype(jnp.float32)
        return picked.reshape(tok_dev, top_count, width)

    outgoing = fill_slots(tokens[owner])
    weighted = (combine.reshape(-1)[:, None] * cotangent[owner].astype(jnp.float32)).astype(
        jnp.bfloat16
    )
    arrived = lax.all_to_all(outgoing, "expert", split_axis=0, concat_axis=0, tiled=True)
    rows = arrived.reshape(-1, width)
    gate_w = w_gate[0]
    up_w = w_up[0]
    down_w = w_down[0]
    gate = jnp.dot(rows, gate_w, preferred_element_type=jnp.float32)
    up = jnp.dot(rows, up_w, preferred_element_type=jnp.float32)
    sig = jax.nn.sigmoid(gate)
    act = gate * sig
    hidden = (act * up).astype(jnp.bfloat16)
    produced = contract_last(hidden, down_w).astype(jnp.bfloat16).reshape(arrived.shape)
    returned = lax.all_to_all(produced, "expert", split_axis=0, concat_axis=0, tiled=True)
    mixed = jnp.sum(collect(returned) * combine[:, :, None], axis=1).astype(jnp.bfloat16)
    grad_arrived = lax.all_to_all(
        fill_slots(weighted), "expert", split_axis=0, concat_axis=0, tiled=True
    )
    grad_rows = grad_arrived.reshape(-1, width)
    dhidden = jnp.dot(grad_rows, down_w, preferred_element_type=jnp.float32)
    dgate = (dhidden * up * sig * (1.0 + gate * (1.0 - sig))).astype(jnp.bfloat16)
    dup = (dhidden * act).astype(jnp.bfloat16)
    dinput = (contract_last(dgate, gate_w) + contract_last(dup, up_w)).astype(jnp.bfloat16)
    back = lax.all_to_all(
        dinput.reshape(arrived.shape), "expert", split_axis=0, concat_axis=0, tiled=True
    )
    grad_tokens = jnp.sum(collect(back), axis=1).astype(jnp.bfloat16)
    summed = lax.psum_scatter(
        jnp.concatenate(
            [
                contract_first(rows, dgate),
                contract_first(rows, dup),
                contract_first(grad_rows, hidden),
            ],
            axis=1,
        ).astype(jnp.bfloat16),
        "dp",
        scatter_dimension=0,
        tiled=True,
    ).astype(jnp.float32)
    hidden_units = gate_w.shape[1]
    grad_gate = summed[:, :hidden_units].astype(jnp.bfloat16)[None]
    grad_up = summed[:, hidden_units : 2 * hidden_units].astype(jnp.bfloat16)[None]
    grad_down = summed[:, 2 * hidden_units :].astype(jnp.bfloat16)[None]
    return (mixed, grad_tokens, grad_gate, grad_up, grad_down)


VMEM = pltpu.VMEM
LIMIT = 14 * 1024 * 1024


K = {'far0': 0, 'mate': 'T3', 'mate_after': 'T1', 'f3': 't4', 'b2': 'm3', 'b3': 'm4', 'force': 0, 'cot1': 'join'}
COST = {'pair_forward': 30, 'forward_0': 31, 'forward_4': 32, 'backward_0': 31, 'grad_sums_0': 29, 'forward_2': 31, 'grad_sums_1': 30, 'stage': 30, 'mixed_sums_2': 29, 'backward_1': 30, 'join_1': 30}


def call(name, body, outs, operands, smem=0, scratch=(), near=True, far=False):
    specs = [pl.BlockSpec(memory_space=pltpu.SMEM)] * smem
    specs += [pl.BlockSpec(memory_space=pltpu.HBM if far else VMEM)] * (len(operands) - smem)
    if far:
        operands = [pltpu.with_memory_space_constraint(a, pltpu.HBM) for a in operands]
    with jax.named_scope(name):
        return pl.pallas_call(
            body,
            out_shape=[pltpu.VMEM(a.shape, a.dtype) if near else a for a in outs],
            in_specs=specs,
            out_specs=[pl.BlockSpec(memory_space=VMEM)] * len(outs),
            scratch_shapes=list(scratch),
            compiler_params=pltpu.CompilerParams(vmem_limit_bytes=LIMIT),
            cost_estimate=pl.CostEstimate(
                flops=1 << COST.get(name, 20), bytes_accessed=1 << 10, transcendentals=0
            ),
        )(*operands)


def picks(place, cap):
    slots = lax.broadcasted_iota(jnp.int32, (cap, place.shape[1]), 0).astype(F32)
    return jnp.where(slots == place, 1.0, 0.0)


def joined(parts):
    return parts[0] if len(parts) == 1 else jnp.concatenate(parts, axis=0)


def payload_body(routes_hbm, combine_hbm, tokens_hbm, out_ref, routes_ref, combine_ref, sems):
    top, tok = routes_ref.shape
    head = 2 * top
    body = pltpu.make_async_copy(tokens_hbm, out_ref.at[pl.ds(head, tok)], sems.at[0])
    names = pltpu.make_async_copy(routes_hbm, routes_ref, sems.at[1])
    shares = pltpu.make_async_copy(combine_hbm, combine_ref, sems.at[2])
    names.start()
    shares.start()
    body.start()
    out_ref[:head] = jnp.zeros((head, out_ref.shape[1]), BF16)
    names.wait()
    shares.wait()
    exact = combine_ref[...]
    high = exact.astype(BF16)
    rest = exact - high.astype(F32)
    middle = rest.astype(BF16)
    low = (rest - middle.astype(F32)).astype(BF16)
    blank = jnp.zeros((top, tok), F32)
    named = jnp.concatenate([routes_ref[...].astype(F32), high.astype(F32)], axis=0)
    out_ref[:head, :tok] = named.astype(BF16)
    for i, term in enumerate((middle, low)):
        padded = jnp.concatenate([blank, term.astype(F32)], axis=0)
        out_ref[:head, (i + 1) * tok : (i + 2) * tok] = padded.astype(BF16)
    body.wait()


def join_body(head, tok, first, second, out):
    if head:
        reach = 3 * tok
        out[:head] = first[:head]
        out[:head, 4 * tok : 4 * tok + reach] = second[:head, :reach]
    out[head : head + tok] = first[head:]
    out[head + tok :] = second[head:]


def stage_body(*refs):
    *pairs, sems = refs
    half = len(pairs) // 2
    copies = [
        pltpu.make_async_copy(pairs[i], pairs[half + i], sems.at[i]) for i in range(half)
    ]
    for copy in copies:
        copy.start()
    for copy in copies:
        copy.wait()


def told_of(side, j, head, tok):
    told = side[:head, 4 * tok * j : 4 * tok * j + 3 * tok].astype(F32)
    names, told = told[: head // 2, :tok], told[head // 2 :]
    return names, told[:, :tok] + (told[:, tok : 2 * tok] + told[:, 2 * tok :])


def places_of(wanted, info_ref):
    masks, weights = [], []
    for names, terms, expert in wanted:
        hit = names == expert
        masks.append(jnp.sum(jnp.where(hit, 1.0, 0.0), axis=0, keepdims=True))
        weights.append(jnp.sum(jnp.where(hit, terms, 0.0), axis=0, keepdims=True))
    tok = info_ref.shape[1]
    pad = jnp.zeros((8 - len(masks), tok), F32)
    mask = jnp.concatenate(masks + [pad], axis=0)
    before = lax.broadcasted_iota(jnp.int32, (tok, tok), 0) < lax.broadcasted_iota(
        jnp.int32, (tok, tok), 1
    )
    rank = jnp.dot(
        mask.astype(BF16), jnp.where(before, 1.0, 0.0).astype(BF16), preferred_element_type=F32
    )
    place = jnp.where(mask > 0.5, rank, -1.0)
    info_ref[0:8] = place
    info_ref[8:16] = jnp.concatenate(weights + [pad], axis=0)
    return place, weights


def hidden_of(rows, w_gate, w_up):
    gate = jnp.dot(rows, w_gate[...], preferred_element_type=F32)
    up = jnp.dot(rows, w_up[...], preferred_element_type=F32)
    sig = jax.nn.sigmoid(gate)
    act = gate * sig
    return (act * up).astype(BF16), up * sig * (1.0 + gate * (1.0 - sig)), act


def forward_body(cap, top, kept, sums, expert_ref, near, far, w_gate, w_up, w_down, *outs):
    info_ref, rows_ref, slope_ref, act_ref, hidden_ref = outs[:5]
    me = expert_ref[0].astype(F32)
    mate = expert_ref[1].astype(F32)
    head = 2 * top
    tok = info_ref.shape[1]
    blocks = [(side, j) for side in (near, far) for j in range((side.shape[0] - head) // tok)]
    told = [told_of(side, j, head, tok) for side, j in blocks]
    wanted = [(*t, me) for t in told] + [(*told[i], mate) for i in kept]
    place, weights = places_of(wanted, info_ref)
    share = []
    for i, (side, j) in enumerate(blocks):
        low = head + j * tok
        pick = picks(place[i : i + 1], cap)
        share.append(jnp.sum(pick * weights[i], axis=1, keepdims=True))
        taken = jnp.dot(pick.astype(BF16), side[low : low + tok], preferred_element_type=F32)
        rows_ref[i * cap : (i + 1) * cap] = taken.astype(BF16)
    hidden, slope, act = hidden_of(rows_ref[...], w_gate, w_up)
    hidden_ref[...] = hidden
    slope_ref[...] = slope
    act_ref[...] = act
    if sums:
        produced = contract_last(hidden, w_down[...]).astype(BF16).astype(F32)
        split(kept, cap, (jnp.concatenate(share, axis=0) * produced).astype(BF16), *outs[5:])


def pair_forward_body(cap, top, expert_ref, near, *refs):
    weights, (info_ref, slope_ref, act_ref, out) = refs[:6], refs[6:]
    head = 2 * top
    tok = info_ref.shape[1]
    told = told_of(near, 0, head, tok)
    place, share = places_of([(*told, expert_ref[i].astype(F32)) for i in range(2)], info_ref)
    pick = jnp.concatenate([picks(place[i : i + 1], cap) for i in range(2)], axis=0).astype(BF16)
    rows = jnp.dot(pick, near[head : head + tok], preferred_element_type=F32).astype(BF16)
    sent = []
    for i in range(2):
        w_gate, w_up, w_down = weights[3 * i : 3 * i + 3]
        part = slice(i * cap, (i + 1) * cap)
        hidden, slope_ref[part], act_ref[part] = hidden_of(rows[part], w_gate, w_up)
        produced = contract_last(hidden, w_down[...]).astype(BF16).astype(F32)
        column = jnp.sum(picks(place[i : i + 1], cap) * share[i], axis=1, keepdims=True)
        sent.append((column * produced).astype(BF16))
    out[...] = contract_first(pick, jnp.concatenate(sent, axis=0)).astype(BF16)


def pair_backward_body(cap, info_ref, slope_ref, act_ref, near, *refs):
    weights, out = refs[:6], refs[6]
    pick = [picks(info_ref[i : i + 1], cap) for i in range(2)]
    both = jnp.concatenate(pick, axis=0).astype(BF16)
    taken = jnp.dot(both, near[...], preferred_element_type=F32)
    sent = []
    for i in range(2):
        w_gate, w_up, w_down = weights[3 * i : 3 * i + 3]
        part = slice(i * cap, (i + 1) * cap)
        column = jnp.sum(pick[i] * info_ref[8 + i : 9 + i], axis=1, keepdims=True)
        rows = (column * taken[part]).astype(BF16)
        dhidden = jnp.dot(rows, w_down[...], preferred_element_type=F32)
        dgate = (dhidden * slope_ref[part]).astype(BF16)
        dup = (dhidden * act_ref[part]).astype(BF16)
        back = contract_last(dgate, w_gate[...]) + contract_last(dup, w_up[...])
        sent.append(back.astype(BF16))
    out[...] = contract_first(both, jnp.concatenate(sent, axis=0)).astype(BF16)


def split(kept, cap, rows, keep_ref, give_ref):
    cut = rows.shape[0] // 2
    first, second = (keep_ref, give_ref) if kept[0] == 0 else (give_ref, keep_ref)
    first[...] = rows[:cut]
    second[...] = rows[cut:]


def backward_body(cap, kept, sums, info_ref, slope, act, near, far, w_gate, w_up, w_down, *outs):
    rows_ref, dgate_ref, dup_ref = outs[:3]
    tok = info_ref.shape[1]
    blocks = [(side, low) for side in (near, far) for low in range(0, side.shape[0], tok)]
    for i, (side, low) in enumerate(blocks):
        pick = picks(info_ref[i : i + 1], cap)
        share = jnp.sum(pick * info_ref[8 + i : 9 + i], axis=1, keepdims=True)
        taken = jnp.dot(pick.astype(BF16), side[low : low + tok], preferred_element_type=F32)
        rows_ref[i * cap : (i + 1) * cap] = (share * taken).astype(BF16)
    dhidden = jnp.dot(rows_ref[...], w_down[...], preferred_element_type=F32)
    dgate = (dhidden * slope[...]).astype(BF16)
    dup = (dhidden * act[...]).astype(BF16)
    dgate_ref[...] = dgate
    dup_ref[...] = dup
    if sums:
        back = contract_last(dgate, w_gate[...]) + contract_last(dup, w_up[...])
        split(kept, cap, back.astype(BF16), *outs[3:])


def return_body(cap, kept, count, info_ref, keep, give, *refs):
    arrived, outs = refs[: len(refs) - count], refs[len(refs) - count :]
    tok = info_ref.shape[1]
    sums = []
    for j in reversed(range(len(kept))):
        i = kept[j]
        mate = 2 * len(kept) + j
        both = jnp.concatenate(
            [picks(info_ref[i : i + 1], cap), picks(info_ref[mate : mate + 1], cap)], axis=0
        ).astype(BF16)
        part = slice(j * cap, (j + 1) * cap)
        sums.append(contract_first(both, jnp.concatenate([keep[part], give[part]], axis=0)))
    for ref in arrived:
        for j in range(ref.shape[0] // tok):
            sums[j] = sums[j] + ref[j * tok : (j + 1) * tok].astype(F32)
    for out, total in zip(outs, sums if count > 1 else [joined(sums)]):
        out[...] = total.astype(BF16)


def weights_body(steps, cols, *refs):
    rows = refs[:steps]
    grads = refs[steps : 2 * steps]
    out = refs[2 * steps]
    right = jnp.concatenate([g[...] for g in grads], axis=0)
    for low in range(0, out.shape[0], cols):
        left = jnp.concatenate([r[:, low : low + cols] for r in rows], axis=0)
        out[low : low + cols] = contract_first(left, right).astype(BF16)


def by_ring(tokens, cotangent, routes, combine, w_gate, w_up, w_down):
    tok, width = tokens.shape
    top = routes.shape[1]
    n = lax.axis_size("expert")
    cap = (tok * top + n - 1) // n
    units = w_gate.shape[2]
    gate_w, up_w, down_w = w_gate[0], w_up[0], w_down[0]
    pairs = n // 2
    reach = pairs // 2
    walk = [2 * i for i in range(reach)] + [2 * i + 1 for i in reversed(range(reach))]
    straight = [
        (2 * walk[i] + core, 2 * walk[(i + 1 - 2 * core) % pairs] + core)
        for i in range(pairs)
        for core in range(2)
    ]
    crossing = [
        (2 * walk[i] + core, 2 * walk[(i - 1 + 2 * core) % pairs] + 1 - core)
        for i in range(pairs)
        for core in range(2)
    ]
    crossing_back = [(a, b ^ 1) for a, b in straight]

    def hop(value, what, moves=straight):
        with jax.named_scope(what):
            return lax.ppermute(value, "expert", moves)

    def swap(value, what):
        return hop(value, what, [(i, i ^ 1) for i in range(n)])

    def after(value, *others):
        return lax.optimization_barrier((value, *others))[0] if others else value

    def land(values, *before):
        return list(lax.optimization_barrier((*values, *before))[: len(values)])

    def struct(shape, dtype):
        return jax.ShapeDtypeStruct(shape, dtype)

    here = lax.axis_index("expert").astype(jnp.int32)
    expert = jnp.stack([here, here ^ 1])
    head = 2 * top

    def blocks_of(step):
        return (4, (2, 3)) if 0 < step < reach else (2, (0,))

    forward, backward = {}, {}

    def run_forward(step):
        count, kept = blocks_of(step)
        m = count * cap
        sums = step < reach
        forward[step] = call(
            f"forward_{step}",
            functools.partial(forward_body, cap, top, kept, sums),
            [
                struct((16, tok), F32),
                struct((m, width), BF16),
                struct((m, units), F32),
                struct((m, units), F32),
                struct((m, units), BF16),
            ]
            + [struct((m // 2, width), BF16)] * 2 * sums,
            [expert, token_near[step], token_far[step], gate_w, up_w, down_w],
            smem=1,
        )
        return forward[step][4]

    def run_backward(step):
        count, kept = blocks_of(step)
        m = count * cap
        sums = step < reach
        info, _, slope, act = forward[step][:4]
        backward[step] = call(
            f"backward_{step}",
            functools.partial(backward_body, cap, kept, sums),
            [
                struct((m, width), BF16),
                struct((m, units), BF16),
                struct((m, units), BF16),
            ]
            + [struct((m // 2, width), BF16)] * 2 * sums,
            [info, slope, act, cot_near[step], cot_far[step], gate_w, up_w, down_w],
        )
        return backward[step][1]

    def run_after(run, near, step, *others):
        near[step] = after(near[step], *others)
        return run(step)

    payload = call(
        "payload",
        payload_body,
        [struct((head + tok, width), BF16)],
        [routes.T, combine.T, tokens],
        scratch=[VMEM((top, tok), jnp.int32), VMEM((top, tok), F32), pltpu.SemaphoreType.DMA((3,))],
        far=True,
    )[0]
    staged = after((gate_w, up_w, down_w), payload)
    gate_w, up_w, down_w = call(
        "stage",
        stage_body,
        [struct(w.shape, BF16) for w in staged],
        staged,
        scratch=[pltpu.SemaphoreType.DMA((3,))],
        far=True,
    )

    def join(arrived, top_rows, name):
        if len(arrived) == 1:
            return arrived[0]
        return call(
            name,
            functools.partial(join_body, top_rows, tok),
            [struct((top_rows + 2 * tok, width), BF16)],
            arrived,
        )[0]

    def onward(near, step, top_rows, what):
        if step == reach:
            near = near[: top_rows + tok]
        return [hop(near, f"{what}_{step}")]

    token_near, cot_near = {0: payload}, {0: cotangent}
    token_fly = [hop(payload, "tokens_1"), hop(payload, "tokens_1_crossing", crossing)]
    token_far = {0: swap(payload, "tokens_0_swap")}
    cot_far = {0: swap(after(cotangent, payload), "cotangent_0_swap")}
    if K["cot1"] == "join":
        cot_fly = [hop(join([cotangent, cot_far[0]], 0, "join_0"), "cotangent_1")]
    else:
        late = after(cotangent, payload)
        cot_fly = [hop(late, "cotangent_1"), hop(late, "cotangent_1_crossing", crossing)]

    def mates(where):
        return mate_w if K["mate"] == where else []

    mate_w = []
    for step in range(1, reach):
        before = [backward[step - 2][1]] if step > 1 else [gate_w]
        if step == 1 and K["far0"]:
            before.append(token_far[0])
        if K["force"] and step > 1:
            before.append(cot_far[step - 1])
        *arrived, token_near[step - 1] = land(
            [*token_fly, token_near[step - 1]], *before, *mates(f"T{step}")
        )
        token_near[step] = join(arrived, head, "join_1")
        token_fly = onward(token_near[step], step + 1, head, "tokens")
        token_far[step] = swap(token_near[step], f"tokens_{step}_swap")
        if step == 1:
            first = {"T1": token_near[1], "P": payload, "T0": token_far[0]}[K["mate_after"]]
            mate_w = [swap(after(w, first), "weights_swap") for w in (gate_w, up_w, down_w)]
        before = [run_forward(step - 1)]
        if step == reach - 1 and K["f3"] == "c3":
            before.append(run_forward(step))
        if K["force"]:
            before.append(token_far[step])
        *arrived, cot_near[step - 1] = land(
            [*cot_fly, cot_near[step - 1]], *before, *mates(f"C{step}")
        )
        cot_near[step] = join(arrived, 0, "join_2")
        cot_fly = onward(cot_near[step], step + 1, 0, "cotangent")
        cot_far[step] = swap(cot_near[step], f"cotangent_{step}_swap")
        if step < reach - 1:
            run_backward(step - 1)

    last = reach - 1
    both_w = [gate_w, up_w, down_w, *mate_w]
    before = []
    if K["b2"] == "t4":
        before.append(run_backward(last - 1))
    if K["f3"] == "t4":
        before.append(run_after(run_forward, token_near, last, cot_near[last]))
    if K["force"]:
        before.append(cot_far[last])
    token_near[reach] = land(token_fly, *(before or [cot_near[last]]), *mates(f"T{reach}"))[0]
    info, slope, act, mixed_left = call(
        "pair_forward",
        functools.partial(pair_forward_body, cap, top),
        [
            struct((16, tok), F32),
            struct((2 * cap, units), F32),
            struct((2 * cap, units), F32),
            struct((tok, width), BF16),
        ],
        [expert, token_near[reach], *both_w],
        smem=1,
    )
    mixed_left, mixed_fly = [mixed_left], [hop(mixed_left, f"mixed_{reach}")]
    before = [mixed_left[0]]
    if K["f3"] == "late":
        before.append(run_after(run_forward, token_near, last, *mixed_left))
    if K["b2"] == "c4":
        before.append(run_after(run_backward, cot_near, last - 1, *mixed_left))
    cot_near[reach] = land(cot_fly, *before)[0]
    grad_left = call(
        "pair_backward",
        functools.partial(pair_backward_body, cap),
        [struct((tok, width), BF16)],
        [info, slope, act, cot_near[reach], *both_w],
    )
    grad_fly = [hop(grad_left[0], f"grad_{reach}")]
    before = [*grad_left]
    if K["f3"] == "y":
        before.append(run_after(run_forward, token_near, last, *grad_left))
    if K["b2"] == "m4":
        before.append(run_after(run_backward, cot_near, last - 1, *grad_left))
    if K["b3"] == "m4":
        before.append(run_after(run_backward, cot_near, last, *grad_left))

    def back_from(step, what, kept, given, values):
        outs = {0: (tok,), 1: (tok, tok)}.get(step, (2 * tok,))
        return call(
            f"{what}_sums_{step}",
            functools.partial(return_body, cap, blocks_of(step)[1], len(outs)),
            [struct((rows, width), BF16) for rows in outs],
            [forward[step][0], kept, given, *values],
            near=step > 0,
        )

    def send_back(sums, step, what):
        if step == 1:
            return [hop(sums[0], what + "_1"), hop(sums[1], what + "_1_crossing", crossing_back)]
        return [hop(sums[0], f"{what}_{step}")]

    def mixed_back(step, values):
        given = swap(forward[step][6], f"mixed_{step}_swap")
        return back_from(step, "mixed", forward[step][5], given, values)

    def grad_back(step, values):
        given = swap(backward[step][4], f"grad_{step}_swap")
        return back_from(step, "grad", backward[step][3], given, values)

    grads = []

    def some_job():
        steps = range(reach + 1)
        token_rows = [forward[i][1] for i in steps]
        jobs = [
            (token_rows, [backward[i][1] for i in steps]),
            (token_rows, [backward[i][2] for i in steps]),
            ([backward[i][0] for i in steps], [forward[i][4] for i in steps]),
        ]
        if len(grads) == len(jobs):
            return []
        lefts, rights = jobs[len(grads)]
        grads.extend(call(
            f"weights_{len(grads)}",
            functools.partial(weights_body, len(lefts), 256),
            [struct((width, units), BF16)],
            [*lefts, *rights],
            near=False,
        ))
        return grads[-1:]

    for step in range(last, 0, -1):
        arrived = land(mixed_fly, *before)
        mixed_left = mixed_back(step, arrived)
        mixed_fly = send_back(mixed_left, step, "mixed")
        before = [*mixed_left]
        if step == last:
            if K["b3"] == "m3":
                before.append(run_after(run_backward, cot_near, last, *mixed_left))
            if K["b2"] == "m3":
                before.append(run_after(run_backward, cot_near, last - 1, *mixed_left))
            token_near[reach] = after(token_near[reach], *mixed_left)
            token_far[reach] = swap(token_near[reach], f"tokens_{reach}_swap")
            cot_far[reach] = swap(after(cot_near[reach], *mixed_left), f"cotangent_{reach}_swap")
        else:
            before += some_job()
        arrived = land(grad_fly, *before)
        grad_left = grad_back(step, arrived)
        grad_fly = send_back(grad_left, step, "grad")
        before = [*grad_left]
        if step == last:
            if K["b2"] == "g3":
                before.append(run_after(run_backward, cot_near, last - 1, *grad_left))
            cot_near[reach] = after(cot_near[reach], *grad_left)
            before += [run_forward(reach), run_backward(reach)]
        before += some_job()
    while some_job():
        pass
    arrived = land(mixed_fly, *before, *grads)
    mixed = mixed_back(0, arrived)[0]
    arrived = land(grad_fly, mixed)
    grad_tokens = grad_back(0, arrived)[0]
    return (mixed, grad_tokens, *[g[None] for g in grads])


def per_device(tokens, cotangent, routes, combine, w_gate, w_up, w_down):
    n = lax.axis_size("expert")
    tok, width = tokens.shape
    top = routes.shape[1]
    ring = (
        lax.axis_size("dp") == 1
        and w_gate.shape[0] == 1
        and n % 4 == 0
        and n >= 8
        and n <= 2 * top
        and tok % 128 == 0
        and top % 8 == 0
        and width >= 8 * tok
        and (tok * top) % (16 * n) == 0
    )
    plan = by_ring if ring else by_all_to_all
    return plan(tokens, cotangent, routes, combine, w_gate, w_up, w_down)


def solution(mesh):
    placed = (
        P(("groups", "expert", "dp"), None),
        P(("groups", "expert", "dp"), None),
        P(("groups", "expert", "dp"), None),
        P(("groups", "expert", "dp"), None),
        P("expert", None, None),
        P("expert", None, None),
        P("expert", None, None),
    )
    return jax.shard_map(
        per_device,
        mesh=mesh,
        in_specs=placed,
        out_specs=(
            P(("groups", "expert", "dp"), None),
            P(("groups", "expert", "dp"), None),
            P(("groups", "expert"), "dp", None),
            P(("groups", "expert"), "dp", None),
            P(("groups", "expert"), "dp", None),
        ),
        check_vma=False,
    )
```

```python
import functools

import jax
import jax.numpy as jnp
from jax import lax
from jax.experimental import pallas as pl
from jax.experimental.pallas import tpu as pltpu
from jax.sharding import PartitionSpec as P

F32 = jnp.float32
BF16 = jnp.bfloat16


def contract_last(left, right):
    return lax.dot_general(
        left, right, (((1,), (1,)), ((), ())), preferred_element_type=jnp.float32
    )


def contract_first(left, right):
    return lax.dot_general(
        left, right, (((0,), (0,)), ((), ())), preferred_element_type=jnp.float32
    )


def by_all_to_all(tokens, cotangent, routes, combine, w_gate, w_up, w_down):
    tok_dev, width = tokens.shape
    top_count = routes.shape[1]
    experts = w_gate.shape[0] * lax.axis_size("expert")
    capacity = min(tok_dev, max(2, (tok_dev * top_count + experts - 1) // experts))
    flat = routes.reshape(-1)
    onehot = (flat[:, None] == jnp.arange(experts, dtype=jnp.int32)[None, :]).astype(jnp.int32)
    rank = jnp.cumsum(onehot, axis=0) - onehot
    place = flat * capacity + jnp.sum(rank * onehot, axis=1)
    owner = jnp.arange(tok_dev * top_count, dtype=jnp.int32) // top_count

    def fill_slots(values):
        empty = jnp.zeros((experts * capacity, width), jnp.bfloat16)
        return empty.at[place].set(values).reshape(experts, capacity, width)

    def collect(returned):
        picked = returned.reshape(-1, width)[place].astype(jnp.float32)
        return picked.reshape(tok_dev, top_count, width)

    outgoing = fill_slots(tokens[owner])
    weighted = (combine.reshape(-1)[:, None] * cotangent[owner].astype(jnp.float32)).astype(
        jnp.bfloat16
    )
    arrived = lax.all_to_all(outgoing, "expert", split_axis=0, concat_axis=0, tiled=True)
    rows = arrived.reshape(-1, width)
    gate_w = w_gate[0]
    up_w = w_up[0]
    down_w = w_down[0]
    gate = jnp.dot(rows, gate_w, preferred_element_type=jnp.float32)
    up = jnp.dot(rows, up_w, preferred_element_type=jnp.float32)
    sig = jax.nn.sigmoid(gate)
    act = gate * sig
    hidden = (act * up).astype(jnp.bfloat16)
    produced = contract_last(hidden, down_w).astype(jnp.bfloat16).reshape(arrived.shape)
    returned = lax.all_to_all(produced, "expert", split_axis=0, concat_axis=0, tiled=True)
    mixed = jnp.sum(collect(returned) * combine[:, :, None], axis=1).astype(jnp.bfloat16)
    grad_arrived = lax.all_to_all(
        fill_slots(weighted), "expert", split_axis=0, concat_axis=0, tiled=True
    )
    grad_rows = grad_arrived.reshape(-1, width)
    dhidden = jnp.dot(grad_rows, down_w, preferred_element_type=jnp.float32)
    dgate = (dhidden * up * sig * (1.0 + gate * (1.0 - sig))).astype(jnp.bfloat16)
    dup = (dhidden * act).astype(jnp.bfloat16)
    dinput = (contract_last(dgate, gate_w) + contract_last(dup, up_w)).astype(jnp.bfloat16)
    back = lax.all_to_all(
        dinput.reshape(arrived.shape), "expert", split_axis=0, concat_axis=0, tiled=True
    )
    grad_tokens = jnp.sum(collect(back), axis=1).astype(jnp.bfloat16)
    summed = lax.psum_scatter(
        jnp.concatenate(
            [
                contract_first(rows, dgate),
                contract_first(rows, dup),
                contract_first(grad_rows, hidden),
            ],
            axis=1,
        ).astype(jnp.bfloat16),
        "dp",
        scatter_dimension=0,
        tiled=True,
    ).astype(jnp.float32)
    hidden_units = gate_w.shape[1]
    grad_gate = summed[:, :hidden_units].astype(jnp.bfloat16)[None]
    grad_up = summed[:, hidden_units : 2 * hidden_units].astype(jnp.bfloat16)[None]
    grad_down = summed[:, 2 * hidden_units :].astype(jnp.bfloat16)[None]
    return (mixed, grad_tokens, grad_gate, grad_up, grad_down)


VMEM = pltpu.VMEM
LIMIT = 14 * 1024 * 1024


COST = {
    "pair_forward": 30,
    "forward_0": 32,
    "backward_0": 31,
    "grad_sums_0": 29,
    "forward_2": 32,
    "grad_sums_1": 30,
    "stage": 30,
    "pair_backward": 28,
    "mixed_sums_2": 29,
    "backward_1": 30,
    "join_1": 30,
    "grad_sums_2": 28,
    "payload": 31,
    "mixed_sums_3": 32,
}


def call(name, body, outs, operands, smem=0, scratch=(), near=True, far=False):
    specs = [pl.BlockSpec(memory_space=pltpu.SMEM)] * smem
    specs += [pl.BlockSpec(memory_space=pltpu.HBM if far else VMEM)] * (len(operands) - smem)
    if far:
        operands = [pltpu.with_memory_space_constraint(a, pltpu.HBM) for a in operands]
    with jax.named_scope(name):
        return pl.pallas_call(
            body,
            out_shape=[pltpu.VMEM(a.shape, a.dtype) if near else a for a in outs],
            in_specs=specs,
            out_specs=[pl.BlockSpec(memory_space=VMEM)] * len(outs),
            scratch_shapes=list(scratch),
            compiler_params=pltpu.CompilerParams(vmem_limit_bytes=LIMIT),
            cost_estimate=pl.CostEstimate(
                flops=1 << COST.get(name, 20), bytes_accessed=1 << 10, transcendentals=0
            ),
        )(*operands)


def picks(place, cap):
    slots = lax.broadcasted_iota(jnp.int32, (cap, place.shape[1]), 0).astype(F32)
    return jnp.where(slots == place, 1.0, 0.0)


def joined(parts):
    return parts[0] if len(parts) == 1 else jnp.concatenate(parts, axis=0)


def payload_body(routes_hbm, combine_hbm, tokens_hbm, out_ref, routes_ref, combine_ref, sems):
    top, tok = routes_ref.shape
    head = 2 * top
    body = pltpu.make_async_copy(tokens_hbm, out_ref.at[pl.ds(head, tok)], sems.at[0])
    names = pltpu.make_async_copy(routes_hbm, routes_ref, sems.at[1])
    shares = pltpu.make_async_copy(combine_hbm, combine_ref, sems.at[2])
    names.start()
    shares.start()
    body.start()
    out_ref[:head] = jnp.zeros((head, out_ref.shape[1]), BF16)
    names.wait()
    shares.wait()
    exact = combine_ref[...]
    high = exact.astype(BF16)
    rest = exact - high.astype(F32)
    middle = rest.astype(BF16)
    low = (rest - middle.astype(F32)).astype(BF16)
    blank = jnp.zeros((top, tok), F32)
    named = jnp.concatenate([routes_ref[...].astype(F32), high.astype(F32)], axis=0)
    out_ref[:head, :tok] = named.astype(BF16)
    for i, term in enumerate((middle, low)):
        padded = jnp.concatenate([blank, term.astype(F32)], axis=0)
        out_ref[:head, (i + 1) * tok : (i + 2) * tok] = padded.astype(BF16)
    body.wait()


def join_body(head, tok, first, second, out):
    if head:
        reach = 3 * tok
        out[:head] = first[:head]
        out[:head, 4 * tok : 4 * tok + reach] = second[:head, :reach]
    out[head : head + tok] = first[head:]
    out[head + tok :] = second[head:]


def stage_body(*refs):
    *pairs, sems = refs
    half = len(pairs) // 2
    copies = [
        pltpu.make_async_copy(pairs[i], pairs[half + i], sems.at[i]) for i in range(half)
    ]
    for copy in copies:
        copy.start()
    for copy in copies:
        copy.wait()


def told_of(side, j, head, tok):
    told = side[:head, 4 * tok * j : 4 * tok * j + 3 * tok].astype(F32)
    names, told = told[: head // 2, :tok], told[head // 2 :]
    return names, told[:, :tok] + (told[:, tok : 2 * tok] + told[:, 2 * tok :])


def places_of(wanted, info_ref):
    masks, weights = [], []
    for names, terms, expert in wanted:
        hit = names == expert
        masks.append(jnp.sum(jnp.where(hit, 1.0, 0.0), axis=0, keepdims=True))
        weights.append(jnp.sum(jnp.where(hit, terms, 0.0), axis=0, keepdims=True))
    tok = info_ref.shape[1]
    pad = jnp.zeros((8 - len(masks), tok), F32)
    mask = jnp.concatenate(masks + [pad], axis=0)
    before = lax.broadcasted_iota(jnp.int32, (tok, tok), 0) < lax.broadcasted_iota(
        jnp.int32, (tok, tok), 1
    )
    rank = jnp.dot(
        mask.astype(BF16), jnp.where(before, 1.0, 0.0).astype(BF16), preferred_element_type=F32
    )
    place = jnp.where(mask > 0.5, rank, -1.0)
    info_ref[0:8] = place
    info_ref[8:16] = jnp.concatenate(weights + [pad], axis=0)
    return place, weights


def hidden_of(rows, w_gate, w_up):
    gate = jnp.dot(rows, w_gate[...], preferred_element_type=F32)
    up = jnp.dot(rows, w_up[...], preferred_element_type=F32)
    sig = jax.nn.sigmoid(gate)
    act = gate * sig
    return (act * up).astype(BF16), up * sig * (1.0 + gate * (1.0 - sig)), act


def forward_body(cap, top, kept, sums, expert_ref, near, far, w_gate, w_up, w_down, *outs):
    info_ref, rows_ref, slope_ref, act_ref, hidden_ref = outs[:5]
    me = expert_ref[0].astype(F32)
    mate = expert_ref[1].astype(F32)
    head = 2 * top
    tok = info_ref.shape[1]
    blocks = [(side, j) for side in (near, far) for j in range((side.shape[0] - head) // tok)]
    told = [told_of(side, j, head, tok) for side, j in blocks]
    wanted = [(*t, me) for t in told] + [(*told[i], mate) for i in kept]
    place, weights = places_of(wanted, info_ref)
    share = []
    for i, (side, j) in enumerate(blocks):
        low = head + j * tok
        pick = picks(place[i : i + 1], cap)
        share.append(jnp.sum(pick * weights[i], axis=1, keepdims=True))
        taken = jnp.dot(pick.astype(BF16), side[low : low + tok], preferred_element_type=F32)
        rows_ref[i * cap : (i + 1) * cap] = taken.astype(BF16)
    hidden, slope, act = hidden_of(rows_ref[...], w_gate, w_up)
    hidden_ref[...] = hidden
    slope_ref[...] = slope
    act_ref[...] = act
    if sums:
        produced = contract_last(hidden, w_down[...]).astype(BF16).astype(F32)
        split(kept, cap, (jnp.concatenate(share, axis=0) * produced).astype(BF16), *outs[5:])


def pair_forward_body(cap, top, expert_ref, near, *refs):
    weights, (info_ref, slope_ref, act_ref, out) = refs[:6], refs[6:]
    head = 2 * top
    tok = info_ref.shape[1]
    told = told_of(near, 0, head, tok)
    place, share = places_of([(*told, expert_ref[i].astype(F32)) for i in range(2)], info_ref)
    pick = jnp.concatenate([picks(place[i : i + 1], cap) for i in range(2)], axis=0).astype(BF16)
    rows = jnp.dot(pick, near[head : head + tok], preferred_element_type=F32).astype(BF16)
    sent = []
    for i in range(2):
        w_gate, w_up, w_down = weights[3 * i : 3 * i + 3]
        part = slice(i * cap, (i + 1) * cap)
        hidden, slope_ref[part], act_ref[part] = hidden_of(rows[part], w_gate, w_up)
        produced = contract_last(hidden, w_down[...]).astype(BF16).astype(F32)
        column = jnp.sum(picks(place[i : i + 1], cap) * share[i], axis=1, keepdims=True)
        sent.append((column * produced).astype(BF16))
    out[...] = contract_first(pick, jnp.concatenate(sent, axis=0)).astype(BF16)


def pair_backward_body(cap, info_ref, slope_ref, act_ref, near, *refs):
    weights, out = refs[:6], refs[6]
    pick = [picks(info_ref[i : i + 1], cap) for i in range(2)]
    both = jnp.concatenate(pick, axis=0).astype(BF16)
    taken = jnp.dot(both, near[...], preferred_element_type=F32)
    sent = []
    for i in range(2):
        w_gate, w_up, w_down = weights[3 * i : 3 * i + 3]
        part = slice(i * cap, (i + 1) * cap)
        column = jnp.sum(pick[i] * info_ref[8 + i : 9 + i], axis=1, keepdims=True)
        rows = (column * taken[part]).astype(BF16)
        dhidden = jnp.dot(rows, w_down[...], preferred_element_type=F32)
        dgate = (dhidden * slope_ref[part]).astype(BF16)
        dup = (dhidden * act_ref[part]).astype(BF16)
        back = contract_last(dgate, w_gate[...]) + contract_last(dup, w_up[...])
        sent.append(back.astype(BF16))
    out[...] = contract_first(both, jnp.concatenate(sent, axis=0)).astype(BF16)


def split(kept, cap, rows, keep_ref, give_ref):
    cut = rows.shape[0] // 2
    first, second = (keep_ref, give_ref) if kept[0] == 0 else (give_ref, keep_ref)
    first[...] = rows[:cut]
    second[...] = rows[cut:]


def backward_body(cap, kept, sums, info_ref, slope, act, near, far, w_gate, w_up, w_down, *outs):
    rows_ref, dgate_ref, dup_ref = outs[:3]
    tok = info_ref.shape[1]
    blocks = [(side, low) for side in (near, far) for low in range(0, side.shape[0], tok)]
    for i, (side, low) in enumerate(blocks):
        pick = picks(info_ref[i : i + 1], cap)
        share = jnp.sum(pick * info_ref[8 + i : 9 + i], axis=1, keepdims=True)
        taken = jnp.dot(pick.astype(BF16), side[low : low + tok], preferred_element_type=F32)
        rows_ref[i * cap : (i + 1) * cap] = (share * taken).astype(BF16)
    dhidden = jnp.dot(rows_ref[...], w_down[...], preferred_element_type=F32)
    dgate = (dhidden * slope[...]).astype(BF16)
    dup = (dhidden * act[...]).astype(BF16)
    dgate_ref[...] = dgate
    dup_ref[...] = dup
    if sums:
        back = contract_last(dgate, w_gate[...]) + contract_last(dup, w_up[...])
        split(kept, cap, back.astype(BF16), *outs[3:])


def return_body(cap, kept, count, info_ref, keep, give, *refs):
    arrived, outs = refs[: len(refs) - count], refs[len(refs) - count :]
    tok = info_ref.shape[1]
    sums = []
    for j in reversed(range(len(kept))):
        i = kept[j]
        mate = 2 * len(kept) + j
        both = jnp.concatenate(
            [picks(info_ref[i : i + 1], cap), picks(info_ref[mate : mate + 1], cap)], axis=0
        ).astype(BF16)
        part = slice(j * cap, (j + 1) * cap)
        sums.append(contract_first(both, jnp.concatenate([keep[part], give[part]], axis=0)))
    for ref in arrived:
        for j in range(ref.shape[0] // tok):
            sums[j] = sums[j] + ref[j * tok : (j + 1) * tok].astype(F32)
    for out, total in zip(outs, sums if count > 1 else [joined(sums)]):
        out[...] = total.astype(BF16)


def weights_body(steps, cols, *refs):
    rows = refs[:steps]
    grads = refs[steps : 2 * steps]
    out = refs[2 * steps]
    right = jnp.concatenate([g[...] for g in grads], axis=0)
    for low in range(0, out.shape[0], cols):
        left = jnp.concatenate([r[:, low : low + cols] for r in rows], axis=0)
        out[low : low + cols] = contract_first(left, right).astype(BF16)


def by_ring(tokens, cotangent, routes, combine, w_gate, w_up, w_down):
    tok, width = tokens.shape
    top = routes.shape[1]
    n = lax.axis_size("expert")
    cap = (tok * top + n - 1) // n
    units = w_gate.shape[2]
    gate_w, up_w, down_w = w_gate[0], w_up[0], w_down[0]
    pairs = n // 2
    reach = pairs // 2
    walk = [2 * i for i in range(reach)] + [2 * i + 1 for i in reversed(range(reach))]
    straight = [
        (2 * walk[i] + core, 2 * walk[(i + 1 - 2 * core) % pairs] + core)
        for i in range(pairs)
        for core in range(2)
    ]
    crossing = [
        (2 * walk[i] + core, 2 * walk[(i - 1 + 2 * core) % pairs] + 1 - core)
        for i in range(pairs)
        for core in range(2)
    ]
    crossing_back = [(a, b ^ 1) for a, b in straight]

    def hop(value, what, moves=straight):
        with jax.named_scope(what):
            return lax.ppermute(value, "expert", moves)

    def swap(value, what):
        return hop(value, what, [(i, i ^ 1) for i in range(n)])

    def after(value, *others):
        return lax.optimization_barrier((value, *others))[0] if others else value

    def land(values, *before):
        return list(lax.optimization_barrier((*values, *before))[: len(values)])

    def struct(shape, dtype):
        return jax.ShapeDtypeStruct(shape, dtype)

    here = lax.axis_index("expert").astype(jnp.int32)
    expert = jnp.stack([here, here ^ 1])
    head = 2 * top

    def blocks_of(step):
        return (4, (2, 3)) if 0 < step < reach else (2, (0,))

    forward, backward = {}, {}

    def run_forward(step):
        count, kept = blocks_of(step)
        m = count * cap
        sums = step < reach
        forward[step] = call(
            f"forward_{step}",
            functools.partial(forward_body, cap, top, kept, sums),
            [
                struct((16, tok), F32),
                struct((m, width), BF16),
                struct((m, units), F32),
                struct((m, units), F32),
                struct((m, units), BF16),
            ]
            + [struct((m // 2, width), BF16)] * 2 * sums,
            [expert, token_near[step], token_far[step], gate_w, up_w, down_w],
            smem=1,
        )
        return forward[step][4]

    def run_backward(step):
        count, kept = blocks_of(step)
        m = count * cap
        sums = step < reach
        info, _, slope, act = forward[step][:4]
        backward[step] = call(
            f"backward_{step}",
            functools.partial(backward_body, cap, kept, sums),
            [
                struct((m, width), BF16),
                struct((m, units), BF16),
                struct((m, units), BF16),
            ]
            + [struct((m // 2, width), BF16)] * 2 * sums,
            [info, slope, act, cot_near[step], cot_far[step], gate_w, up_w, down_w],
        )
        return backward[step][1]

    def run_after(run, near, step, *others):
        near[step] = after(near[step], *others)
        return run(step)

    payload = call(
        "payload",
        payload_body,
        [struct((head + tok, width), BF16)],
        [routes.T, combine.T, tokens],
        scratch=[VMEM((top, tok), jnp.int32), VMEM((top, tok), F32), pltpu.SemaphoreType.DMA((3,))],
        far=True,
    )[0]
    staged = after((gate_w, up_w, down_w), payload)
    gate_w, up_w, down_w = call(
        "stage",
        stage_body,
        [struct(w.shape, BF16) for w in staged],
        staged,
        scratch=[pltpu.SemaphoreType.DMA((3,))],
        far=True,
    )

    def join(arrived, top_rows, name):
        if len(arrived) == 1:
            return arrived[0]
        return call(
            name,
            functools.partial(join_body, top_rows, tok),
            [struct((top_rows + 2 * tok, width), BF16)],
            arrived,
        )[0]

    def onward(near, step, top_rows, what):
        if step == reach:
            near = near[: top_rows + tok]
        return [hop(near, f"{what}_{step}")]

    token_near, cot_near = {0: payload}, {0: cotangent}
    token_fly = [hop(payload, "tokens_1"), hop(payload, "tokens_1_crossing", crossing)]
    token_far = {0: swap(payload, "tokens_0_swap")}
    cot_far = {0: swap(after(cotangent, payload), "cotangent_0_swap")}
    cot_fly = [hop(join([cotangent, cot_far[0]], 0, "join_0"), "cotangent_1")]
    mate_w = []
    for step in range(1, reach):
        before = [backward[step - 2][1]] if step > 1 else [gate_w]
        *arrived, token_near[step - 1] = land(
            [*token_fly, token_near[step - 1]], *before, *(mate_w if step == 3 else [])
        )
        token_near[step] = join(arrived, head, "join_1")
        token_fly = onward(token_near[step], step + 1, head, "tokens")
        token_far[step] = swap(token_near[step], f"tokens_{step}_swap")
        if step == 1:
            mate_w = [swap(after(w, token_near[1]), "weights_swap") for w in (gate_w, up_w, down_w)]
        done = run_forward(step - 1)
        *arrived, cot_near[step - 1] = land([*cot_fly, cot_near[step - 1]], done)
        cot_near[step] = join(arrived, 0, "join_2")
        cot_fly = onward(cot_near[step], step + 1, 0, "cotangent")
        cot_far[step] = swap(cot_near[step], f"cotangent_{step}_swap")
        if step < reach - 1:
            run_backward(step - 1)

    last = reach - 1
    both_w = [gate_w, up_w, down_w, *mate_w]
    done = run_after(run_forward, token_near, last, cot_near[last])
    token_near[reach] = land(token_fly, done)[0]
    info, slope, act, mixed_left = call(
        "pair_forward",
        functools.partial(pair_forward_body, cap, top),
        [
            struct((16, tok), F32),
            struct((2 * cap, units), F32),
            struct((2 * cap, units), F32),
            struct((tok, width), BF16),
        ],
        [expert, token_near[reach], *both_w],
        smem=1,
    )
    mixed_left, mixed_fly = [mixed_left], [hop(mixed_left, f"mixed_{reach}")]
    cot_near[reach] = land(cot_fly, *mixed_left)[0]
    grad_left = call(
        "pair_backward",
        functools.partial(pair_backward_body, cap),
        [struct((tok, width), BF16)],
        [info, slope, act, cot_near[reach], *both_w],
    )
    grad_fly = [hop(grad_left[0], f"grad_{reach}")]
    before = [*grad_left, run_after(run_backward, cot_near, last, *grad_left)]

    def back_from(step, what, kept, given, values):
        outs = {0: (tok,), 1: (tok, tok)}.get(step, (2 * tok,))
        return call(
            f"{what}_sums_{step}",
            functools.partial(return_body, cap, blocks_of(step)[1], len(outs)),
            [struct((rows, width), BF16) for rows in outs],
            [forward[step][0], kept, given, *values],
            near=step > 0,
        )

    def send_back(sums, step, what):
        if step == 1:
            return [hop(sums[0], what + "_1"), hop(sums[1], what + "_1_crossing", crossing_back)]
        return [hop(sums[0], f"{what}_{step}")]

    def mixed_back(step, values):
        given = swap(forward[step][6], f"mixed_{step}_swap")
        return back_from(step, "mixed", forward[step][5], given, values)

    def grad_back(step, values):
        given = swap(backward[step][4], f"grad_{step}_swap")
        return back_from(step, "grad", backward[step][3], given, values)

    grads = []

    def some_job():
        steps = range(reach + 1)
        token_rows = [forward[i][1] for i in steps]
        jobs = [
            (token_rows, [backward[i][1] for i in steps]),
            (token_rows, [backward[i][2] for i in steps]),
            ([backward[i][0] for i in steps], [forward[i][4] for i in steps]),
        ]
        if len(grads) == len(jobs):
            return []
        lefts, rights = jobs[len(grads)]
        grads.extend(
            call(
                f"weights_{len(grads)}",
                functools.partial(weights_body, len(lefts), 256),
                [struct((width, units), BF16)],
                [*lefts, *rights],
                near=False,
            )
        )
        return grads[-1:]

    for step in range(last, 0, -1):
        arrived = land(mixed_fly, *before)
        mixed_left = mixed_back(step, arrived)
        mixed_fly = send_back(mixed_left, step, "mixed")
        before = [*mixed_left]
        if step == last:
            before.append(run_after(run_backward, cot_near, last - 1, *mixed_left))
            token_near[reach] = after(token_near[reach], *mixed_left)
            token_far[reach] = swap(token_near[reach], f"tokens_{reach}_swap")
            cot_far[reach] = swap(after(cot_near[reach], *mixed_left), f"cotangent_{reach}_swap")
        else:
            before += some_job()
        arrived = land(grad_fly, *before)
        grad_left = grad_back(step, arrived)
        grad_fly = send_back(grad_left, step, "grad")
        before = [*grad_left]
        if step == last:
            cot_near[reach] = after(cot_near[reach], *grad_left)
            before += [run_forward(reach), run_backward(reach)]
        before += some_job()
    while some_job():
        pass
    arrived = land(mixed_fly, *before, *grads)
    mixed = mixed_back(0, arrived)[0]
    arrived = land(grad_fly, mixed)
    grad_tokens = grad_back(0, arrived)[0]
    return (mixed, grad_tokens, *[g[None] for g in grads])


def per_device(tokens, cotangent, routes, combine, w_gate, w_up, w_down):
    n = lax.axis_size("expert")
    tok, width = tokens.shape
    top = routes.shape[1]
    ring = (
        lax.axis_size("dp") == 1
        and w_gate.shape[0] == 1
        and n % 4 == 0
        and n >= 16
        and n <= 2 * top
        and tok % 128 == 0
        and top % 8 == 0
        and width >= 8 * tok
        and (tok * top) % (16 * n) == 0
    )
    plan = by_ring if ring else by_all_to_all
    return plan(tokens, cotangent, routes, combine, w_gate, w_up, w_down)


def solution(mesh):
    placed = (
        P(("groups", "expert", "dp"), None),
        P(("groups", "expert", "dp"), None),
        P(("groups", "expert", "dp"), None),
        P(("groups", "expert", "dp"), None),
        P("expert", None, None),
        P("expert", None, None),
        P("expert", None, None),
    )
    return jax.shard_map(
        per_device,
        mesh=mesh,
        in_specs=placed,
        out_specs=(
            P(("groups", "expert", "dp"), None),
            P(("groups", "expert", "dp"), None),
            P(("groups", "expert"), "dp", None),
            P(("groups", "expert"), "dp", None),
            P(("groups", "expert"), "dp", None),
        ),
        check_vma=False,
    )
```

```python
import functools

import jax
import jax.numpy as jnp
from jax import lax
from jax.experimental import pallas as pl
from jax.experimental.pallas import tpu as pltpu
from jax.sharding import PartitionSpec as P

F32 = jnp.float32
BF16 = jnp.bfloat16


def contract_last(left, right):
    return lax.dot_general(
        left, right, (((1,), (1,)), ((), ())), preferred_element_type=jnp.float32
    )


def contract_first(left, right):
    return lax.dot_general(
        left, right, (((0,), (0,)), ((), ())), preferred_element_type=jnp.float32
    )


def by_all_to_all(tokens, cotangent, routes, combine, w_gate, w_up, w_down):
    tok_dev, width = tokens.shape
    top_count = routes.shape[1]
    experts = w_gate.shape[0] * lax.axis_size("expert")
    capacity = min(tok_dev, max(2, (tok_dev * top_count + experts - 1) // experts))
    flat = routes.reshape(-1)
    onehot = (flat[:, None] == jnp.arange(experts, dtype=jnp.int32)[None, :]).astype(jnp.int32)
    rank = jnp.cumsum(onehot, axis=0) - onehot
    place = flat * capacity + jnp.sum(rank * onehot, axis=1)
    owner = jnp.arange(tok_dev * top_count, dtype=jnp.int32) // top_count

    def fill_slots(values):
        empty = jnp.zeros((experts * capacity, width), jnp.bfloat16)
        return empty.at[place].set(values).reshape(experts, capacity, width)

    def collect(returned):
        picked = returned.reshape(-1, width)[place].astype(jnp.float32)
        return picked.reshape(tok_dev, top_count, width)

    outgoing = fill_slots(tokens[owner])
    weighted = (combine.reshape(-1)[:, None] * cotangent[owner].astype(jnp.float32)).astype(
        jnp.bfloat16
    )
    arrived = lax.all_to_all(outgoing, "expert", split_axis=0, concat_axis=0, tiled=True)
    rows = arrived.reshape(-1, width)
    gate_w = w_gate[0]
    up_w = w_up[0]
    down_w = w_down[0]
    gate = jnp.dot(rows, gate_w, preferred_element_type=jnp.float32)
    up = jnp.dot(rows, up_w, preferred_element_type=jnp.float32)
    sig = jax.nn.sigmoid(gate)
    act = gate * sig
    hidden = (act * up).astype(jnp.bfloat16)
    produced = contract_last(hidden, down_w).astype(jnp.bfloat16).reshape(arrived.shape)
    returned = lax.all_to_all(produced, "expert", split_axis=0, concat_axis=0, tiled=True)
    mixed = jnp.sum(collect(returned) * combine[:, :, None], axis=1).astype(jnp.bfloat16)
    grad_arrived = lax.all_to_all(
        fill_slots(weighted), "expert", split_axis=0, concat_axis=0, tiled=True
    )
    grad_rows = grad_arrived.reshape(-1, width)
    dhidden = jnp.dot(grad_rows, down_w, preferred_element_type=jnp.float32)
    dgate = (dhidden * up * sig * (1.0 + gate * (1.0 - sig))).astype(jnp.bfloat16)
    dup = (dhidden * act).astype(jnp.bfloat16)
    dinput = (contract_last(dgate, gate_w) + contract_last(dup, up_w)).astype(jnp.bfloat16)
    back = lax.all_to_all(
        dinput.reshape(arrived.shape), "expert", split_axis=0, concat_axis=0, tiled=True
    )
    grad_tokens = jnp.sum(collect(back), axis=1).astype(jnp.bfloat16)
    summed = lax.psum_scatter(
        jnp.concatenate(
            [
                contract_first(rows, dgate),
                contract_first(rows, dup),
                contract_first(grad_rows, hidden),
            ],
            axis=1,
        ).astype(jnp.bfloat16),
        "dp",
        scatter_dimension=0,
        tiled=True,
    ).astype(jnp.float32)
    hidden_units = gate_w.shape[1]
    grad_gate = summed[:, :hidden_units].astype(jnp.bfloat16)[None]
    grad_up = summed[:, hidden_units : 2 * hidden_units].astype(jnp.bfloat16)[None]
    grad_down = summed[:, 2 * hidden_units :].astype(jnp.bfloat16)[None]
    return (mixed, grad_tokens, grad_gate, grad_up, grad_down)


VMEM = pltpu.VMEM
LIMIT = 14 * 1024 * 1024


COST = {
    "pair_forward": 30,
    "forward_0": 32,
    "backward_0": 31,
    "grad_sums_0": 29,
    "forward_2": 32,
    "grad_sums_1": 30,
    "stage": 30,
    "pair_backward": 28,
    "mixed_sums_2": 29,
    "backward_1": 30,
    "join_1": 30,
    "grad_sums_2": 28,
    "payload": 31,
    "mixed_sums_3": 32,
}


def call(name, body, outs, operands, smem=0, scratch=(), near=True, far=False):
    specs = [pl.BlockSpec(memory_space=pltpu.SMEM)] * smem
    specs += [pl.BlockSpec(memory_space=pltpu.HBM if far else VMEM)] * (len(operands) - smem)
    if far:
        operands = [pltpu.with_memory_space_constraint(a, pltpu.HBM) for a in operands]
    with jax.named_scope(name):
        return pl.pallas_call(
            body,
            out_shape=[pltpu.VMEM(a.shape, a.dtype) if near else a for a in outs],
            in_specs=specs,
            out_specs=[pl.BlockSpec(memory_space=VMEM)] * len(outs),
            scratch_shapes=list(scratch),
            compiler_params=pltpu.CompilerParams(vmem_limit_bytes=LIMIT),
            cost_estimate=pl.CostEstimate(
                flops=1 << COST.get(name, 20), bytes_accessed=1 << 10, transcendentals=0
            ),
        )(*operands)


def picks(place, cap):
    slots = lax.broadcasted_iota(jnp.int32, (cap, place.shape[1]), 0).astype(F32)
    return jnp.where(slots == place, 1.0, 0.0)


def joined(parts):
    return parts[0] if len(parts) == 1 else jnp.concatenate(parts, axis=0)


def payload_body(routes_hbm, combine_hbm, tokens_hbm, out_ref, routes_ref, combine_ref, sems):
    top, tok = routes_ref.shape
    head = 2 * top
    body = pltpu.make_async_copy(tokens_hbm, out_ref.at[pl.ds(head, tok)], sems.at[0])
    names = pltpu.make_async_copy(routes_hbm, routes_ref, sems.at[1])
    shares = pltpu.make_async_copy(combine_hbm, combine_ref, sems.at[2])
    names.start()
    shares.start()
    body.start()
    out_ref[:head] = jnp.zeros((head, out_ref.shape[1]), BF16)
    names.wait()
    shares.wait()
    exact = combine_ref[...]
    high = exact.astype(BF16)
    rest = exact - high.astype(F32)
    middle = rest.astype(BF16)
    low = (rest - middle.astype(F32)).astype(BF16)
    blank = jnp.zeros((top, tok), F32)
    named = jnp.concatenate([routes_ref[...].astype(F32), high.astype(F32)], axis=0)
    out_ref[:head, :tok] = named.astype(BF16)
    for i, term in enumerate((middle, low)):
        padded = jnp.concatenate([blank, term.astype(F32)], axis=0)
        out_ref[:head, (i + 1) * tok : (i + 2) * tok] = padded.astype(BF16)
    body.wait()


def join_body(head, tok, first, second, out):
    if head:
        reach = 3 * tok
        out[:head] = first[:head]
        out[:head, 4 * tok : 4 * tok + reach] = second[:head, :reach]
    out[head : head + tok] = first[head:]
    out[head + tok :] = second[head:]


def stage_body(*refs):
    *pairs, sems = refs
    half = len(pairs) // 2
    copies = [
        pltpu.make_async_copy(pairs[i], pairs[half + i], sems.at[i]) for i in range(half)
    ]
    for copy in copies:
        copy.start()
    for copy in copies:
        copy.wait()


def told_of(side, j, head, tok):
    told = side[:head, 4 * tok * j : 4 * tok * j + 3 * tok].astype(F32)
    names, told = told[: head // 2, :tok], told[head // 2 :]
    return names, told[:, :tok] + (told[:, tok : 2 * tok] + told[:, 2 * tok :])


def places_of(wanted, info_ref):
    masks, weights = [], []
    for names, terms, expert in wanted:
        hit = names == expert
        masks.append(jnp.sum(jnp.where(hit, 1.0, 0.0), axis=0, keepdims=True))
        weights.append(jnp.sum(jnp.where(hit, terms, 0.0), axis=0, keepdims=True))
    tok = info_ref.shape[1]
    pad = jnp.zeros((8 - len(masks), tok), F32)
    mask = jnp.concatenate(masks + [pad], axis=0)
    before = lax.broadcasted_iota(jnp.int32, (tok, tok), 0) < lax.broadcasted_iota(
        jnp.int32, (tok, tok), 1
    )
    rank = jnp.dot(
        mask.astype(BF16), jnp.where(before, 1.0, 0.0).astype(BF16), preferred_element_type=F32
    )
    place = jnp.where(mask > 0.5, rank, -1.0)
    info_ref[0:8] = place
    info_ref[8:16] = jnp.concatenate(weights + [pad], axis=0)
    return place, weights


def hidden_of(rows, w_gate, w_up):
    gate = jnp.dot(rows, w_gate[...], preferred_element_type=F32)
    up = jnp.dot(rows, w_up[...], preferred_element_type=F32)
    sig = jax.nn.sigmoid(gate)
    act = gate * sig
    return (act * up).astype(BF16), up * sig * (1.0 + gate * (1.0 - sig)), act


def forward_body(cap, top, kept, sums, expert_ref, near, far, w_gate, w_up, w_down, *outs):
    info_ref, rows_ref, slope_ref, act_ref, hidden_ref = outs[:5]
    me = expert_ref[0].astype(F32)
    mate = expert_ref[1].astype(F32)
    head = 2 * top
    tok = info_ref.shape[1]
    blocks = [(side, j) for side in (near, far) for j in range((side.shape[0] - head) // tok)]
    told = [told_of(side, j, head, tok) for side, j in blocks]
    wanted = [(*t, me) for t in told] + [(*told[i], mate) for i in kept]
    place, weights = places_of(wanted, info_ref)
    share = []
    for i, (side, j) in enumerate(blocks):
        low = head + j * tok
        pick = picks(place[i : i + 1], cap)
        share.append(jnp.sum(pick * weights[i], axis=1, keepdims=True))
        taken = jnp.dot(pick.astype(BF16), side[low : low + tok], preferred_element_type=F32)
        rows_ref[i * cap : (i + 1) * cap] = taken.astype(BF16)
    hidden, slope, act = hidden_of(rows_ref[...], w_gate, w_up)
    hidden_ref[...] = hidden
    slope_ref[...] = slope
    act_ref[...] = act
    if sums:
        produced = contract_last(hidden, w_down[...]).astype(BF16).astype(F32)
        split(kept, cap, (jnp.concatenate(share, axis=0) * produced).astype(BF16), *outs[5:])


def pair_forward_body(cap, top, expert_ref, near, *refs):
    weights, (info_ref, slope_ref, act_ref, out) = refs[:6], refs[6:]
    head = 2 * top
    tok = info_ref.shape[1]
    told = told_of(near, 0, head, tok)
    place, share = places_of([(*told, expert_ref[i].astype(F32)) for i in range(2)], info_ref)
    pick = jnp.concatenate([picks(place[i : i + 1], cap) for i in range(2)], axis=0).astype(BF16)
    rows = jnp.dot(pick, near[head : head + tok], preferred_element_type=F32).astype(BF16)
    sent = []
    for i in range(2):
        w_gate, w_up, w_down = weights[3 * i : 3 * i + 3]
        part = slice(i * cap, (i + 1) * cap)
        hidden, slope_ref[part], act_ref[part] = hidden_of(rows[part], w_gate, w_up)
        produced = contract_last(hidden, w_down[...]).astype(BF16).astype(F32)
        column = jnp.sum(picks(place[i : i + 1], cap) * share[i], axis=1, keepdims=True)
        sent.append((column * produced).astype(BF16))
    out[...] = contract_first(pick, jnp.concatenate(sent, axis=0)).astype(BF16)


def pair_backward_body(cap, info_ref, slope_ref, act_ref, near, *refs):
    weights, out = refs[:6], refs[6]
    pick = [picks(info_ref[i : i + 1], cap) for i in range(2)]
    both = jnp.concatenate(pick, axis=0).astype(BF16)
    taken = jnp.dot(both, near[...], preferred_element_type=F32)
    sent = []
    for i in range(2):
        w_gate, w_up, w_down = weights[3 * i : 3 * i + 3]
        part = slice(i * cap, (i + 1) * cap)
        column = jnp.sum(pick[i] * info_ref[8 + i : 9 + i], axis=1, keepdims=True)
        rows = (column * taken[part]).astype(BF16)
        dhidden = jnp.dot(rows, w_down[...], preferred_element_type=F32)
        dgate = (dhidden * slope_ref[part]).astype(BF16)
        dup = (dhidden * act_ref[part]).astype(BF16)
        back = contract_last(dgate, w_gate[...]) + contract_last(dup, w_up[...])
        sent.append(back.astype(BF16))
    out[...] = contract_first(both, jnp.concatenate(sent, axis=0)).astype(BF16)


def split(kept, cap, rows, keep_ref, give_ref):
    cut = rows.shape[0] // 2
    first, second = (keep_ref, give_ref) if kept[0] == 0 else (give_ref, keep_ref)
    first[...] = rows[:cut]
    second[...] = rows[cut:]


def backward_body(cap, kept, sums, info_ref, slope, act, near, far, w_gate, w_up, w_down, *outs):
    rows_ref, dgate_ref, dup_ref = outs[:3]
    tok = info_ref.shape[1]
    blocks = [(side, low) for side in (near, far) for low in range(0, side.shape[0], tok)]
    for i, (side, low) in enumerate(blocks):
        pick = picks(info_ref[i : i + 1], cap)
        share = jnp.sum(pick * info_ref[8 + i : 9 + i], axis=1, keepdims=True)
        taken = jnp.dot(pick.astype(BF16), side[low : low + tok], preferred_element_type=F32)
        rows_ref[i * cap : (i + 1) * cap] = (share * taken).astype(BF16)
    dhidden = jnp.dot(rows_ref[...], w_down[...], preferred_element_type=F32)
    dgate = (dhidden * slope[...]).astype(BF16)
    dup = (dhidden * act[...]).astype(BF16)
    dgate_ref[...] = dgate
    dup_ref[...] = dup
    if sums:
        back = contract_last(dgate, w_gate[...]) + contract_last(dup, w_up[...])
        split(kept, cap, back.astype(BF16), *outs[3:])


def return_body(cap, kept, count, info_ref, keep, give, *refs):
    arrived, outs = refs[: len(refs) - count], refs[len(refs) - count :]
    tok = info_ref.shape[1]
    sums = []
    for j in reversed(range(len(kept))):
        i = kept[j]
        mate = 2 * len(kept) + j
        both = jnp.concatenate(
            [picks(info_ref[i : i + 1], cap), picks(info_ref[mate : mate + 1], cap)], axis=0
        ).astype(BF16)
        part = slice(j * cap, (j + 1) * cap)
        sums.append(contract_first(both, jnp.concatenate([keep[part], give[part]], axis=0)))
    for ref in arrived:
        for j in range(ref.shape[0] // tok):
            sums[j] = sums[j] + ref[j * tok : (j + 1) * tok].astype(F32)
    for out, total in zip(outs, sums if count > 1 else [joined(sums)]):
        out[...] = total.astype(out.dtype)


def last_body(own, first, second, out):
    out[...] = (own[...] + first[...].astype(F32) + second[...].astype(F32)).astype(BF16)


def weights_body(steps, cols, *refs):
    rows = refs[:steps]
    grads = refs[steps : 2 * steps]
    out = refs[2 * steps]
    right = jnp.concatenate([g[...] for g in grads], axis=0)
    for low in range(0, out.shape[0], cols):
        left = jnp.concatenate([r[:, low : low + cols] for r in rows], axis=0)
        out[low : low + cols] = contract_first(left, right).astype(BF16)


def by_ring(tokens, cotangent, routes, combine, w_gate, w_up, w_down):
    tok, width = tokens.shape
    top = routes.shape[1]
    n = lax.axis_size("expert")
    cap = (tok * top + n - 1) // n
    units = w_gate.shape[2]
    gate_w, up_w, down_w = w_gate[0], w_up[0], w_down[0]
    pairs = n // 2
    reach = pairs // 2
    walk = [2 * i for i in range(reach)] + [2 * i + 1 for i in reversed(range(reach))]
    straight = [
        (2 * walk[i] + core, 2 * walk[(i + 1 - 2 * core) % pairs] + core)
        for i in range(pairs)
        for core in range(2)
    ]
    crossing = [
        (2 * walk[i] + core, 2 * walk[(i - 1 + 2 * core) % pairs] + 1 - core)
        for i in range(pairs)
        for core in range(2)
    ]
    crossing_back = [(a, b ^ 1) for a, b in straight]

    def hop(value, what, moves=straight):
        with jax.named_scope(what):
            return lax.ppermute(value, "expert", moves)

    def swap(value, what):
        return hop(value, what, [(i, i ^ 1) for i in range(n)])

    def after(value, *others):
        return lax.optimization_barrier((value, *others))[0] if others else value

    def land(values, *before):
        return list(lax.optimization_barrier((*values, *before))[: len(values)])

    def struct(shape, dtype):
        return jax.ShapeDtypeStruct(shape, dtype)

    here = lax.axis_index("expert").astype(jnp.int32)
    expert = jnp.stack([here, here ^ 1])
    head = 2 * top

    def blocks_of(step):
        return (4, (2, 3)) if 0 < step < reach else (2, (0,))

    forward, backward = {}, {}

    def run_forward(step):
        count, kept = blocks_of(step)
        m = count * cap
        sums = step < reach
        forward[step] = call(
            f"forward_{step}",
            functools.partial(forward_body, cap, top, kept, sums),
            [
                struct((16, tok), F32),
                struct((m, width), BF16),
                struct((m, units), F32),
                struct((m, units), F32),
                struct((m, units), BF16),
            ]
            + [struct((m // 2, width), BF16)] * 2 * sums,
            [expert, token_near[step], token_far[step], gate_w, up_w, down_w],
            smem=1,
        )
        return forward[step][4]

    def run_backward(step):
        count, kept = blocks_of(step)
        m = count * cap
        sums = step < reach
        info, _, slope, act = forward[step][:4]
        backward[step] = call(
            f"backward_{step}",
            functools.partial(backward_body, cap, kept, sums),
            [
                struct((m, width), BF16),
                struct((m, units), BF16),
                struct((m, units), BF16),
            ]
            + [struct((m // 2, width), BF16)] * 2 * sums,
            [info, slope, act, cot_near[step], cot_far[step], gate_w, up_w, down_w],
        )
        return backward[step][1]

    def run_after(run, near, step, *others):
        near[step] = after(near[step], *others)
        return run(step)

    payload = call(
        "payload",
        payload_body,
        [struct((head + tok, width), BF16)],
        [routes.T, combine.T, tokens],
        scratch=[VMEM((top, tok), jnp.int32), VMEM((top, tok), F32), pltpu.SemaphoreType.DMA((3,))],
        far=True,
    )[0]
    staged = after((gate_w, up_w, down_w), payload)
    gate_w, up_w, down_w = call(
        "stage",
        stage_body,
        [struct(w.shape, BF16) for w in staged],
        staged,
        scratch=[pltpu.SemaphoreType.DMA((3,))],
        far=True,
    )

    def join(arrived, top_rows, name):
        if len(arrived) == 1:
            return arrived[0]
        return call(
            name,
            functools.partial(join_body, top_rows, tok),
            [struct((top_rows + 2 * tok, width), BF16)],
            arrived,
        )[0]

    def onward(near, step, top_rows, what):
        if step == reach:
            near = near[: top_rows + tok]
        return [hop(near, f"{what}_{step}")]

    token_near, cot_near = {0: payload}, {0: cotangent}
    token_fly = [hop(payload, "tokens_1"), hop(payload, "tokens_1_crossing", crossing)]
    token_far = {0: swap(payload, "tokens_0_swap")}
    cot_far = {0: swap(after(cotangent, payload), "cotangent_0_swap")}
    cot_fly = [hop(join([cotangent, cot_far[0]], 0, "join_0"), "cotangent_1")]
    mate_w = []
    for step in range(1, reach):
        before = [backward[step - 2][1]] if step > 1 else [gate_w]
        *arrived, token_near[step - 1] = land(
            [*token_fly, token_near[step - 1]], *before, *(mate_w if step == 3 else [])
        )
        token_near[step] = join(arrived, head, "join_1")
        token_fly = onward(token_near[step], step + 1, head, "tokens")
        token_far[step] = swap(token_near[step], f"tokens_{step}_swap")
        if step == 1:
            mate_w = [swap(after(w, token_near[1]), "weights_swap") for w in (gate_w, up_w, down_w)]
        done = run_forward(step - 1)
        *arrived, cot_near[step - 1] = land([*cot_fly, cot_near[step - 1]], done)
        cot_near[step] = join(arrived, 0, "join_2")
        cot_fly = onward(cot_near[step], step + 1, 0, "cotangent")
        cot_far[step] = swap(cot_near[step], f"cotangent_{step}_swap")
        if step < reach - 1:
            run_backward(step - 1)

    last = reach - 1
    both_w = [gate_w, up_w, down_w, *mate_w]
    done = run_after(run_forward, token_near, last, cot_near[last])
    token_near[reach] = land(token_fly, done)[0]
    info, slope, act, mixed_left = call(
        "pair_forward",
        functools.partial(pair_forward_body, cap, top),
        [
            struct((16, tok), F32),
            struct((2 * cap, units), F32),
            struct((2 * cap, units), F32),
            struct((tok, width), BF16),
        ],
        [expert, token_near[reach], *both_w],
        smem=1,
    )
    mixed_left, mixed_fly = [mixed_left], [hop(mixed_left, f"mixed_{reach}")]
    cot_near[reach] = land(cot_fly, *mixed_left)[0]
    grad_left = call(
        "pair_backward",
        functools.partial(pair_backward_body, cap),
        [struct((tok, width), BF16)],
        [info, slope, act, cot_near[reach], *both_w],
    )
    grad_fly = [hop(grad_left[0], f"grad_{reach}")]
    before = [*grad_left, run_after(run_backward, cot_near, last, *grad_left)]

    def back_from(step, what, kept, given, values):
        outs = {0: (tok,), 1: (tok, tok)}.get(step, (2 * tok,))
        return call(
            f"{what}_sums_{step}",
            functools.partial(return_body, cap, blocks_of(step)[1], len(outs)),
            [struct((rows, width), BF16) for rows in outs],
            [forward[step][0], kept, given, *values],
            near=step > 0,
        )

    def send_back(sums, step, what):
        if step == 1:
            return [hop(sums[0], what + "_1"), hop(sums[1], what + "_1_crossing", crossing_back)]
        return [hop(sums[0], f"{what}_{step}")]

    def mixed_back(step, values):
        given = swap(forward[step][6], f"mixed_{step}_swap")
        return back_from(step, "mixed", forward[step][5], given, values)

    def grad_back(step, values):
        given = swap(backward[step][4], f"grad_{step}_swap")
        return back_from(step, "grad", backward[step][3], given, values)

    grads = []

    def some_job():
        steps = range(reach + 1)
        token_rows = [forward[i][1] for i in steps]
        jobs = [
            (token_rows, [backward[i][1] for i in steps]),
            (token_rows, [backward[i][2] for i in steps]),
            ([backward[i][0] for i in steps], [forward[i][4] for i in steps]),
        ]
        if len(grads) == len(jobs):
            return []
        lefts, rights = jobs[len(grads)]
        grads.extend(
            call(
                f"weights_{len(grads)}",
                functools.partial(weights_body, len(lefts), 256),
                [struct((width, units), BF16)],
                [*lefts, *rights],
                near=False,
            )
        )
        return grads[-1:]

    for step in range(last, 0, -1):
        arrived = land(mixed_fly, *before)
        mixed_left = mixed_back(step, arrived)
        mixed_fly = send_back(mixed_left, step, "mixed")
        before = [*mixed_left]
        if step == last:
            before.append(run_after(run_backward, cot_near, last - 1, *mixed_left))
            token_near[reach] = after(token_near[reach], *mixed_left)
            token_far[reach] = swap(token_near[reach], f"tokens_{reach}_swap")
            cot_far[reach] = swap(after(cot_near[reach], *mixed_left), f"cotangent_{reach}_swap")
        else:
            before += some_job()
        arrived = land(grad_fly, *before)
        grad_left = grad_back(step, arrived)
        grad_fly = send_back(grad_left, step, "grad")
        before = [*grad_left]
        if step == last:
            cot_near[reach] = after(cot_near[reach], *grad_left)
            before += [run_forward(reach), run_backward(reach)]
        before += some_job()
    while some_job():
        pass
    arrived = land(mixed_fly, *before, *grads)
    mixed = mixed_back(0, arrived)[0]
    given = swap(backward[0][4], "grad_0_swap")
    (own,) = call(
        "grad_sums_0",
        functools.partial(return_body, cap, blocks_of(0)[1], 1),
        [struct((tok, width), F32)],
        [forward[0][0], backward[0][3], given],
    )
    arrived = land(grad_fly, mixed, own)
    (grad_tokens,) = call(
        "grad_last", last_body, [struct((tok, width), BF16)], [own, *arrived], near=False
    )
    return (mixed, grad_tokens, *[g[None] for g in grads])


def per_device(tokens, cotangent, routes, combine, w_gate, w_up, w_down):
    n = lax.axis_size("expert")
    tok, width = tokens.shape
    top = routes.shape[1]
    ring = (
        lax.axis_size("dp") == 1
        and w_gate.shape[0] == 1
        and n % 4 == 0
        and n >= 16
        and n <= 2 * top
        and tok % 128 == 0
        and top % 8 == 0
        and width >= 8 * tok
        and (tok * top) % (16 * n) == 0
    )
    plan = by_ring if ring else by_all_to_all
    return plan(tokens, cotangent, routes, combine, w_gate, w_up, w_down)


def solution(mesh):
    placed = (
        P(("groups", "expert", "dp"), None),
        P(("groups", "expert", "dp"), None),
        P(("groups", "expert", "dp"), None),
        P(("groups", "expert", "dp"), None),
        P("expert", None, None),
        P("expert", None, None),
        P("expert", None, None),
    )
    return jax.shard_map(
        per_device,
        mesh=mesh,
        in_specs=placed,
        out_specs=(
            P(("groups", "expert", "dp"), None),
            P(("groups", "expert", "dp"), None),
            P(("groups", "expert"), "dp", None),
            P(("groups", "expert"), "dp", None),
            P(("groups", "expert"), "dp", None),
        ),
        check_vma=False,
    )
```

```python
import functools

import jax
import jax.numpy as jnp
from jax import lax
from jax.experimental import pallas as pl
from jax.experimental.pallas import tpu as pltpu
from jax.sharding import PartitionSpec as P

F32 = jnp.float32
BF16 = jnp.bfloat16


def contract_last(left, right):
    return lax.dot_general(
        left, right, (((1,), (1,)), ((), ())), preferred_element_type=jnp.float32
    )


def contract_first(left, right):
    return lax.dot_general(
        left, right, (((0,), (0,)), ((), ())), preferred_element_type=jnp.float32
    )


def by_all_to_all(tokens, cotangent, routes, combine, w_gate, w_up, w_down):
    tok_dev, width = tokens.shape
    top_count = routes.shape[1]
    experts = w_gate.shape[0] * lax.axis_size("expert")
    capacity = min(tok_dev, max(2, (tok_dev * top_count + experts - 1) // experts))
    flat = routes.reshape(-1)
    onehot = (flat[:, None] == jnp.arange(experts, dtype=jnp.int32)[None, :]).astype(jnp.int32)
    rank = jnp.cumsum(onehot, axis=0) - onehot
    place = flat * capacity + jnp.sum(rank * onehot, axis=1)
    owner = jnp.arange(tok_dev * top_count, dtype=jnp.int32) // top_count

    def fill_slots(values):
        empty = jnp.zeros((experts * capacity, width), jnp.bfloat16)
        return empty.at[place].set(values).reshape(experts, capacity, width)

    def collect(returned):
        picked = returned.reshape(-1, width)[place].astype(jnp.float32)
        return picked.reshape(tok_dev, top_count, width)

    outgoing = fill_slots(tokens[owner])
    weighted = (combine.reshape(-1)[:, None] * cotangent[owner].astype(jnp.float32)).astype(
        jnp.bfloat16
    )
    arrived = lax.all_to_all(outgoing, "expert", split_axis=0, concat_axis=0, tiled=True)
    rows = arrived.reshape(-1, width)
    gate_w = w_gate[0]
    up_w = w_up[0]
    down_w = w_down[0]
    gate = jnp.dot(rows, gate_w, preferred_element_type=jnp.float32)
    up = jnp.dot(rows, up_w, preferred_element_type=jnp.float32)
    sig = jax.nn.sigmoid(gate)
    act = gate * sig
    hidden = (act * up).astype(jnp.bfloat16)
    produced = contract_last(hidden, down_w).astype(jnp.bfloat16).reshape(arrived.shape)
    returned = lax.all_to_all(produced, "expert", split_axis=0, concat_axis=0, tiled=True)
    mixed = jnp.sum(collect(returned) * combine[:, :, None], axis=1).astype(jnp.bfloat16)
    grad_arrived = lax.all_to_all(
        fill_slots(weighted), "expert", split_axis=0, concat_axis=0, tiled=True
    )
    grad_rows = grad_arrived.reshape(-1, width)
    dhidden = jnp.dot(grad_rows, down_w, preferred_element_type=jnp.float32)
    dgate = (dhidden * up * sig * (1.0 + gate * (1.0 - sig))).astype(jnp.bfloat16)
    dup = (dhidden * act).astype(jnp.bfloat16)
    dinput = (contract_last(dgate, gate_w) + contract_last(dup, up_w)).astype(jnp.bfloat16)
    back = lax.all_to_all(
        dinput.reshape(arrived.shape), "expert", split_axis=0, concat_axis=0, tiled=True
    )
    grad_tokens = jnp.sum(collect(back), axis=1).astype(jnp.bfloat16)
    summed = lax.psum_scatter(
        jnp.concatenate(
            [
                contract_first(rows, dgate),
                contract_first(rows, dup),
                contract_first(grad_rows, hidden),
            ],
            axis=1,
        ).astype(jnp.bfloat16),
        "dp",
        scatter_dimension=0,
        tiled=True,
    ).astype(jnp.float32)
    hidden_units = gate_w.shape[1]
    grad_gate = summed[:, :hidden_units].astype(jnp.bfloat16)[None]
    grad_up = summed[:, hidden_units : 2 * hidden_units].astype(jnp.bfloat16)[None]
    grad_down = summed[:, 2 * hidden_units :].astype(jnp.bfloat16)[None]
    return (mixed, grad_tokens, grad_gate, grad_up, grad_down)


VMEM = pltpu.VMEM
LIMIT = 14 * 1024 * 1024


COST = {
    "pair_forward": 30,
    "forward_0": 32,
    "backward_0": 31,
    "grad_sums_0": 29,
    "forward_2": 32,
    "grad_sums_1": 30,
    "stage": 30,
    "pair_backward": 28,
    "mixed_sums_2": 29,
    "backward_1": 30,
    "join_1": 30,
    "grad_sums_2": 28,
    "payload": 31,
    "mixed_sums_3": 32,
}


def call(name, body, outs, operands, smem=0, scratch=(), near=True, far=False):
    specs = [pl.BlockSpec(memory_space=pltpu.SMEM)] * smem
    specs += [pl.BlockSpec(memory_space=pltpu.HBM if far else VMEM)] * (len(operands) - smem)
    if far:
        operands = [pltpu.with_memory_space_constraint(a, pltpu.HBM) for a in operands]
    with jax.named_scope(name):
        return pl.pallas_call(
            body,
            out_shape=[pltpu.VMEM(a.shape, a.dtype) if near else a for a in outs],
            in_specs=specs,
            out_specs=[pl.BlockSpec(memory_space=VMEM)] * len(outs),
            scratch_shapes=list(scratch),
            compiler_params=pltpu.CompilerParams(vmem_limit_bytes=LIMIT),
            cost_estimate=pl.CostEstimate(
                flops=1 << COST.get(name, 20), bytes_accessed=1 << 10, transcendentals=0
            ),
        )(*operands)


def picks(place, cap):
    slots = lax.broadcasted_iota(jnp.int32, (cap, place.shape[1]), 0).astype(F32)
    return jnp.where(slots == place, 1.0, 0.0)


def joined(parts):
    return parts[0] if len(parts) == 1 else jnp.concatenate(parts, axis=0)


def payload_body(routes_hbm, combine_hbm, tokens_hbm, out_ref, routes_ref, combine_ref, sems):
    top, tok = routes_ref.shape
    head = 2 * top
    body = pltpu.make_async_copy(tokens_hbm, out_ref.at[pl.ds(head, tok)], sems.at[0])
    names = pltpu.make_async_copy(routes_hbm, routes_ref, sems.at[1])
    shares = pltpu.make_async_copy(combine_hbm, combine_ref, sems.at[2])
    names.start()
    shares.start()
    body.start()
    out_ref[:head] = jnp.zeros((head, out_ref.shape[1]), BF16)
    names.wait()
    shares.wait()
    exact = combine_ref[...]
    high = exact.astype(BF16)
    rest = exact - high.astype(F32)
    middle = rest.astype(BF16)
    low = (rest - middle.astype(F32)).astype(BF16)
    blank = jnp.zeros((top, tok), F32)
    named = jnp.concatenate([routes_ref[...].astype(F32), high.astype(F32)], axis=0)
    out_ref[:head, :tok] = named.astype(BF16)
    for i, term in enumerate((middle, low)):
        padded = jnp.concatenate([blank, term.astype(F32)], axis=0)
        out_ref[:head, (i + 1) * tok : (i + 2) * tok] = padded.astype(BF16)
    body.wait()


def join_body(head, tok, first, second, out):
    if head:
        reach = 3 * tok
        out[:head] = first[:head]
        out[:head, 4 * tok : 4 * tok + reach] = second[:head, :reach]
    out[head : head + tok] = first[head:]
    out[head + tok :] = second[head:]


def stage_body(*refs):
    *pairs, sems = refs
    half = len(pairs) // 2
    copies = [
        pltpu.make_async_copy(pairs[i], pairs[half + i], sems.at[i]) for i in range(half)
    ]
    for copy in copies:
        copy.start()
    for copy in copies:
        copy.wait()


def told_of(side, j, head, tok):
    told = side[:head, 4 * tok * j : 4 * tok * j + 3 * tok].astype(F32)
    names, told = told[: head // 2, :tok], told[head // 2 :]
    return names, told[:, :tok] + (told[:, tok : 2 * tok] + told[:, 2 * tok :])


def places_of(wanted, info_ref):
    masks, weights = [], []
    for names, terms, expert in wanted:
        hit = names == expert
        masks.append(jnp.sum(jnp.where(hit, 1.0, 0.0), axis=0, keepdims=True))
        weights.append(jnp.sum(jnp.where(hit, terms, 0.0), axis=0, keepdims=True))
    tok = info_ref.shape[1]
    pad = jnp.zeros((8 - len(masks), tok), F32)
    mask = jnp.concatenate(masks + [pad], axis=0)
    before = lax.broadcasted_iota(jnp.int32, (tok, tok), 0) < lax.broadcasted_iota(
        jnp.int32, (tok, tok), 1
    )
    rank = jnp.dot(
        mask.astype(BF16), jnp.where(before, 1.0, 0.0).astype(BF16), preferred_element_type=F32
    )
    place = jnp.where(mask > 0.5, rank, -1.0)
    info_ref[0:8] = place
    info_ref[8:16] = jnp.concatenate(weights + [pad], axis=0)
    return place, weights


def hidden_of(rows, w_gate, w_up):
    gate = jnp.dot(rows, w_gate[...], preferred_element_type=F32)
    up = jnp.dot(rows, w_up[...], preferred_element_type=F32)
    sig = jax.nn.sigmoid(gate)
    act = gate * sig
    return (act * up).astype(BF16), up * sig * (1.0 + gate * (1.0 - sig)), act


def forward_body(cap, top, kept, sums, expert_ref, near, far, w_gate, w_up, w_down, *outs):
    info_ref, rows_ref, slope_ref, act_ref, hidden_ref = outs[:5]
    me = expert_ref[0].astype(F32)
    mate = expert_ref[1].astype(F32)
    head = 2 * top
    tok = info_ref.shape[1]
    blocks = [(side, j) for side in (near, far) for j in range((side.shape[0] - head) // tok)]
    told = [told_of(side, j, head, tok) for side, j in blocks]
    wanted = [(*t, me) for t in told] + [(*told[i], mate) for i in kept]
    place, weights = places_of(wanted, info_ref)
    share = []
    for i, (side, j) in enumerate(blocks):
        low = head + j * tok
        pick = picks(place[i : i + 1], cap)
        share.append(jnp.sum(pick * weights[i], axis=1, keepdims=True))
        taken = jnp.dot(pick.astype(BF16), side[low : low + tok], preferred_element_type=F32)
        rows_ref[i * cap : (i + 1) * cap] = taken.astype(BF16)
    hidden, slope, act = hidden_of(rows_ref[...], w_gate, w_up)
    hidden_ref[...] = hidden
    slope_ref[...] = slope
    act_ref[...] = act
    if sums:
        produced = contract_last(hidden, w_down[...]).astype(BF16).astype(F32)
        split(kept, cap, (jnp.concatenate(share, axis=0) * produced).astype(BF16), *outs[5:])


def pair_forward_body(cap, top, expert_ref, near, *refs):
    weights, (info_ref, slope_ref, act_ref, out) = refs[:6], refs[6:]
    head = 2 * top
    tok = info_ref.shape[1]
    told = told_of(near, 0, head, tok)
    place, share = places_of([(*told, expert_ref[i].astype(F32)) for i in range(2)], info_ref)
    pick = jnp.concatenate([picks(place[i : i + 1], cap) for i in range(2)], axis=0).astype(BF16)
    rows = jnp.dot(pick, near[head : head + tok], preferred_element_type=F32).astype(BF16)
    sent = []
    for i in range(2):
        w_gate, w_up, w_down = weights[3 * i : 3 * i + 3]
        part = slice(i * cap, (i + 1) * cap)
        hidden, slope_ref[part], act_ref[part] = hidden_of(rows[part], w_gate, w_up)
        produced = contract_last(hidden, w_down[...]).astype(BF16).astype(F32)
        column = jnp.sum(picks(place[i : i + 1], cap) * share[i], axis=1, keepdims=True)
        sent.append((column * produced).astype(BF16))
    out[...] = contract_first(pick, jnp.concatenate(sent, axis=0)).astype(BF16)


def pair_backward_body(cap, info_ref, slope_ref, act_ref, near, *refs):
    weights, out = refs[:6], refs[6]
    pick = [picks(info_ref[i : i + 1], cap) for i in range(2)]
    both = jnp.concatenate(pick, axis=0).astype(BF16)
    taken = jnp.dot(both, near[...], preferred_element_type=F32)
    sent = []
    for i in range(2):
        w_gate, w_up, w_down = weights[3 * i : 3 * i + 3]
        part = slice(i * cap, (i + 1) * cap)
        column = jnp.sum(pick[i] * info_ref[8 + i : 9 + i], axis=1, keepdims=True)
        rows = (column * taken[part]).astype(BF16)
        dhidden = jnp.dot(rows, w_down[...], preferred_element_type=F32)
        dgate = (dhidden * slope_ref[part]).astype(BF16)
        dup = (dhidden * act_ref[part]).astype(BF16)
        back = contract_last(dgate, w_gate[...]) + contract_last(dup, w_up[...])
        sent.append(back.astype(BF16))
    out[...] = contract_first(both, jnp.concatenate(sent, axis=0)).astype(BF16)


def split(kept, cap, rows, keep_ref, give_ref):
    cut = rows.shape[0] // 2
    first, second = (keep_ref, give_ref) if kept[0] == 0 else (give_ref, keep_ref)
    first[...] = rows[:cut]
    second[...] = rows[cut:]


def backward_body(cap, kept, sums, info_ref, slope, act, near, far, w_gate, w_up, w_down, *outs):
    rows_ref, dgate_ref, dup_ref = outs[:3]
    tok = info_ref.shape[1]
    blocks = [(side, low) for side in (near, far) for low in range(0, side.shape[0], tok)]
    for i, (side, low) in enumerate(blocks):
        pick = picks(info_ref[i : i + 1], cap)
        share = jnp.sum(pick * info_ref[8 + i : 9 + i], axis=1, keepdims=True)
        taken = jnp.dot(pick.astype(BF16), side[low : low + tok], preferred_element_type=F32)
        rows_ref[i * cap : (i + 1) * cap] = (share * taken).astype(BF16)
    dhidden = jnp.dot(rows_ref[...], w_down[...], preferred_element_type=F32)
    dgate = (dhidden * slope[...]).astype(BF16)
    dup = (dhidden * act[...]).astype(BF16)
    dgate_ref[...] = dgate
    dup_ref[...] = dup
    if sums:
        back = contract_last(dgate, w_gate[...]) + contract_last(dup, w_up[...])
        split(kept, cap, back.astype(BF16), *outs[3:])


def return_body(cap, kept, count, info_ref, keep, give, *refs):
    arrived, outs = refs[: len(refs) - count], refs[len(refs) - count :]
    tok = info_ref.shape[1]
    sums = []
    for j in reversed(range(len(kept))):
        i = kept[j]
        mate = 2 * len(kept) + j
        both = jnp.concatenate(
            [picks(info_ref[i : i + 1], cap), picks(info_ref[mate : mate + 1], cap)], axis=0
        ).astype(BF16)
        part = slice(j * cap, (j + 1) * cap)
        sums.append(contract_first(both, jnp.concatenate([keep[part], give[part]], axis=0)))
    for ref in arrived:
        for j in range(ref.shape[0] // tok):
            sums[j] = sums[j] + ref[j * tok : (j + 1) * tok].astype(F32)
    for out, total in zip(outs, sums if count > 1 else [joined(sums)]):
        out[...] = total.astype(BF16)


def weights_body(steps, cols, *refs):
    rows = refs[:steps]
    grads = refs[steps : 2 * steps]
    out = refs[2 * steps]
    right = jnp.concatenate([g[...] for g in grads], axis=0)
    for low in range(0, out.shape[0], cols):
        left = jnp.concatenate([r[:, low : low + cols] for r in rows], axis=0)
        out[low : low + cols] = contract_first(left, right).astype(BF16)


def by_ring(tokens, cotangent, routes, combine, w_gate, w_up, w_down):
    tok, width = tokens.shape
    top = routes.shape[1]
    n = lax.axis_size("expert")
    cap = (tok * top + n - 1) // n
    units = w_gate.shape[2]
    gate_w, up_w, down_w = w_gate[0], w_up[0], w_down[0]
    pairs = n // 2
    reach = pairs // 2
    walk = [2 * i for i in range(reach)] + [2 * i + 1 for i in reversed(range(reach))]
    straight = [
        (2 * walk[i] + core, 2 * walk[(i + 1 - 2 * core) % pairs] + core)
        for i in range(pairs)
        for core in range(2)
    ]
    crossing = [
        (2 * walk[i] + core, 2 * walk[(i - 1 + 2 * core) % pairs] + 1 - core)
        for i in range(pairs)
        for core in range(2)
    ]
    crossing_back = [(a, b ^ 1) for a, b in straight]

    def hop(value, what, moves=straight):
        with jax.named_scope(what):
            return lax.ppermute(value, "expert", moves)

    def swap(value, what):
        return hop(value, what, [(i, i ^ 1) for i in range(n)])

    def after(value, *others):
        return lax.optimization_barrier((value, *others))[0] if others else value

    def land(values, *before):
        return list(lax.optimization_barrier((*values, *before))[: len(values)])

    def struct(shape, dtype):
        return jax.ShapeDtypeStruct(shape, dtype)

    here = lax.axis_index("expert").astype(jnp.int32)
    expert = jnp.stack([here, here ^ 1])
    head = 2 * top

    def blocks_of(step):
        return (4, (2, 3)) if 0 < step < reach else (2, (0,))

    forward, backward = {}, {}

    def run_forward(step):
        count, kept = blocks_of(step)
        m = count * cap
        sums = step < reach
        forward[step] = call(
            f"forward_{step}",
            functools.partial(forward_body, cap, top, kept, sums),
            [
                struct((16, tok), F32),
                struct((m, width), BF16),
                struct((m, units), F32),
                struct((m, units), F32),
                struct((m, units), BF16),
            ]
            + [struct((m // 2, width), BF16)] * 2 * sums,
            [expert, token_near[step], token_far[step], gate_w, up_w, down_w],
            smem=1,
        )
        return forward[step][4]

    def run_backward(step):
        count, kept = blocks_of(step)
        m = count * cap
        sums = step < reach
        info, _, slope, act = forward[step][:4]
        backward[step] = call(
            f"backward_{step}",
            functools.partial(backward_body, cap, kept, sums),
            [
                struct((m, width), BF16),
                struct((m, units), BF16),
                struct((m, units), BF16),
            ]
            + [struct((m // 2, width), BF16)] * 2 * sums,
            [info, slope, act, cot_near[step], cot_far[step], gate_w, up_w, down_w],
        )
        return backward[step][1]

    def run_after(run, near, step, *others):
        near[step] = after(near[step], *others)
        return run(step)

    payload = call(
        "payload",
        payload_body,
        [struct((head + tok, width), BF16)],
        [routes.T, combine.T, tokens],
        scratch=[VMEM((top, tok), jnp.int32), VMEM((top, tok), F32), pltpu.SemaphoreType.DMA((3,))],
        far=True,
    )[0]
    staged = after((gate_w, up_w, down_w), payload)
    gate_w, up_w, down_w = call(
        "stage",
        stage_body,
        [struct(w.shape, BF16) for w in staged],
        staged,
        scratch=[pltpu.SemaphoreType.DMA((3,))],
        far=True,
    )

    def join(arrived, top_rows, name):
        if len(arrived) == 1:
            return arrived[0]
        return call(
            name,
            functools.partial(join_body, top_rows, tok),
            [struct((top_rows + 2 * tok, width), BF16)],
            arrived,
        )[0]

    def onward(near, step, top_rows, what):
        if step == reach:
            near = near[: top_rows + tok]
        return [hop(near, f"{what}_{step}")]

    token_near, cot_near = {0: payload}, {0: cotangent}
    token_fly = [hop(payload, "tokens_1"), hop(payload, "tokens_1_crossing", crossing)]
    token_far = {0: swap(payload, "tokens_0_swap")}
    cot_far = {0: swap(after(cotangent, payload), "cotangent_0_swap")}
    cot_fly = [hop(join([cotangent, cot_far[0]], 0, "join_0"), "cotangent_1")]
    mate_w = []
    for step in range(1, reach):
        before = [backward[step - 2][1]] if step > 1 else [gate_w]
        *arrived, token_near[step - 1] = land(
            [*token_fly, token_near[step - 1]], *before, *(mate_w if step == 3 else [])
        )
        token_near[step] = join(arrived, head, "join_1")
        token_fly = onward(token_near[step], step + 1, head, "tokens")
        token_far[step] = swap(token_near[step], f"tokens_{step}_swap")
        if step == 1:
            mate_w = [swap(after(w, token_near[1]), "weights_swap") for w in (gate_w, up_w, down_w)]
        done = run_forward(step - 1)
        *arrived, cot_near[step - 1] = land([*cot_fly, cot_near[step - 1]], done)
        cot_near[step] = join(arrived, 0, "join_2")
        cot_fly = onward(cot_near[step], step + 1, 0, "cotangent")
        cot_far[step] = swap(cot_near[step], f"cotangent_{step}_swap")
        if step < reach - 1:
            run_backward(step - 1)

    last = reach - 1
    both_w = [gate_w, up_w, down_w, *mate_w]
    done = run_after(run_forward, token_near, last, cot_near[last])
    token_near[reach] = land(token_fly, done)[0]
    info, slope, act, mixed_left = call(
        "pair_forward",
        functools.partial(pair_forward_body, cap, top),
        [
            struct((16, tok), F32),
            struct((2 * cap, units), F32),
            struct((2 * cap, units), F32),
            struct((tok, width), BF16),
        ],
        [expert, token_near[reach], *both_w],
        smem=1,
    )
    mixed_left, mixed_fly = [mixed_left], [hop(mixed_left, f"mixed_{reach}")]
    cot_near[reach] = land(cot_fly, *mixed_left)[0]
    grad_left = call(
        "pair_backward",
        functools.partial(pair_backward_body, cap),
        [struct((tok, width), BF16)],
        [info, slope, act, cot_near[reach], *both_w],
    )
    grad_fly = [hop(grad_left[0], f"grad_{reach}")]
    before = [*grad_left, run_after(run_backward, cot_near, last, *grad_left)]

    def back_from(step, what, kept, given, values):
        outs = {0: (tok,), 1: (tok, tok)}.get(step, (2 * tok,))
        return call(
            f"{what}_sums_{step}",
            functools.partial(return_body, cap, blocks_of(step)[1], len(outs)),
            [struct((rows, width), BF16) for rows in outs],
            [forward[step][0], kept, given, *values],
            near=step > 0,
        )

    def send_back(sums, step, what):
        if step == 1:
            return [hop(sums[0], what + "_1"), hop(sums[1], what + "_1_crossing", crossing_back)]
        return [hop(sums[0], f"{what}_{step}")]

    def mixed_back(step, values):
        given = swap(forward[step][6], f"mixed_{step}_swap")
        return back_from(step, "mixed", forward[step][5], given, values)

    def grad_back(step, values):
        given = swap(backward[step][4], f"grad_{step}_swap")
        return back_from(step, "grad", backward[step][3], given, values)

    grads = []

    def some_job():
        steps = range(reach + 1)
        token_rows = [forward[i][1] for i in steps]
        jobs = [
            (token_rows, [backward[i][1] for i in steps]),
            (token_rows, [backward[i][2] for i in steps]),
            ([backward[i][0] for i in steps], [forward[i][4] for i in steps]),
        ]
        if len(grads) == len(jobs):
            return []
        lefts, rights = jobs[len(grads)]
        grads.extend(
            call(
                f"weights_{len(grads)}",
                functools.partial(weights_body, len(lefts), 256),
                [struct((width, units), BF16)],
                [*lefts, *rights],
                near=False,
            )
        )
        return grads[-1:]

    for step in range(last, 0, -1):
        arrived = land(mixed_fly, *before)
        mixed_left = mixed_back(step, arrived)
        mixed_fly = send_back(mixed_left, step, "mixed")
        before = [*mixed_left]
        if step == last:
            before.append(run_after(run_backward, cot_near, last - 1, *mixed_left))
            token_near[reach] = after(token_near[reach], *mixed_left)
            token_far[reach] = swap(token_near[reach], f"tokens_{reach}_swap")
            cot_far[reach] = swap(after(cot_near[reach], *mixed_left), f"cotangent_{reach}_swap")
        else:
            before += some_job()
        arrived = land(grad_fly, *before)
        grad_left = grad_back(step, arrived)
        grad_fly = send_back(grad_left, step, "grad")
        before = [*grad_left]
        if step == last:
            cot_near[reach] = after(cot_near[reach], *grad_left)
            before += [run_forward(reach), run_backward(reach)]
        else:
            before += some_job()
    while some_job():
        pass
    arrived = land(mixed_fly, *before, *grads)
    mixed = mixed_back(0, arrived)[0]
    arrived = land(grad_fly, mixed)
    grad_tokens = grad_back(0, arrived)[0]
    return (mixed, grad_tokens, *[g[None] for g in grads])


def per_device(tokens, cotangent, routes, combine, w_gate, w_up, w_down):
    n = lax.axis_size("expert")
    tok, width = tokens.shape
    top = routes.shape[1]
    ring = (
        lax.axis_size("dp") == 1
        and w_gate.shape[0] == 1
        and n % 4 == 0
        and n >= 16
        and n <= 2 * top
        and tok % 128 == 0
        and top % 8 == 0
        and width >= 8 * tok
        and (tok * top) % (16 * n) == 0
    )
    plan = by_ring if ring else by_all_to_all
    return plan(tokens, cotangent, routes, combine, w_gate, w_up, w_down)


def solution(mesh):
    placed = (
        P(("groups", "expert", "dp"), None),
        P(("groups", "expert", "dp"), None),
        P(("groups", "expert", "dp"), None),
        P(("groups", "expert", "dp"), None),
        P("expert", None, None),
        P("expert", None, None),
        P("expert", None, None),
    )
    return jax.shard_map(
        per_device,
        mesh=mesh,
        in_specs=placed,
        out_specs=(
            P(("groups", "expert", "dp"), None),
            P(("groups", "expert", "dp"), None),
            P(("groups", "expert"), "dp", None),
            P(("groups", "expert"), "dp", None),
            P(("groups", "expert"), "dp", None),
        ),
        check_vma=False,
    )
```
